256 devices in a mesh: axial: 8 (over z_lo, x), sector: 32 (over y, z_hi, core).
Axes of the slice: x: 4, y: 4, z: 8 (z_hi: 4, z_lo: 2; z = z_hi * 2 + z_lo), core: 2. Of those that a mesh axis runs over, the one named last changes fastest.
Arguments:
- state: float32 [5, 6, 6, 6, 8, 32, 128], P(None, None, None, None, 'axial', 'sector'), may hold values from -0.6 to 0.6
- register: float32 [5, 6, 6, 6, 8, 32, 128], P(None, None, None, None, 'axial', 'sector'), may hold values from -6 to 6
- flux_x: float32 [5, 5], replicated, may hold values from -2.5 to 2.5
- flux_y: float32 [5, 5], replicated, may hold values from -2.5 to 2.5
- flux_z: float32 [5, 5], replicated, may hold values from -2.5 to 2.5
- viscosity: float32 [5], replicated, may hold values from 0.01 to 0.1
- mortar_partner: int32 [2, 32], P(None, 'sector'), may hold values from 0 to 31, as said below
Outputs:
- state_new: float32 [5, 6, 6, 6, 8, 32, 128], P(None, None, None, None, 'axial', 'sector')
- register_new: float32 [5, 6, 6, 6, 8, 32, 128], P(None, None, None, None, 'axial', 'sector')
The draws below stay inside these ranges and needn't reach their ends.
Inputs may be any that keep to these rules, and one draw needn't show every extreme that they name: The interface is a rotation by one whole number s of elements plus half an element: mortar_partner[0, c] = (c + s) mod 32 and mortar_partner[1, c] = (c - s - 1) mod 32 for every c, with the same s in both rows.
All inputs are finite; a program needn't handle non-finite values.
Results may differ from the reference program's by a relative error of at most 0.0003.
Values sent between devices are 32-bit elements; how exact they have to be, the bound alone decides.
A program may use at most 64 MiB of HBM per device.

```python
import math
import jax
import jax.numpy as jnp
import numpy as np
from jax import lax

NV = 5
NN = 6
EY = 1
EZ = 128
NXE = 8
NYE = 32
N_SECTOR = 32


def draw_mortar_partner(key, part):
    key = jax.random.fold_in(key, 7)
    total = EY * N_SECTOR
    offset = jax.random.randint(key, (), 0, total, dtype=jnp.int32)
    places = jnp.arange(total, dtype=jnp.int32)
    rotor_row = (places + offset) % total
    stator_row = (places - offset - 1) % total
    return jnp.stack([rotor_row, stator_row]).astype(jnp.int32)


def level_of(own_key, shape, shards, smallest, top_value):
    level, own = 1.0, jax.random.fold_in(own_key, 6)
    for dim, blocks in shards:
        draws = jnp.exp(jax.random.uniform(jax.random.fold_in(own, dim), (blocks,), jnp.float32, smallest / len(shards), top_value / len(shards)))
        level = level * jnp.repeat(draws, shape[dim] // blocks).reshape([-1 if axis == dim else 1 for axis in range(len(shape))])
    return level


def scatter_about(stream_key, extent, scale, reach, shards=(), kind=jnp.bfloat16):
    values = jax.random.normal(stream_key, extent, jnp.float32) * scale
    if len(shards) > 0:
        values = level_of(stream_key, extent, shards, -0.22, 0.18) * values
    return jnp.clip(values, min=-reach, max=reach).astype(kind)


def setup_inputs(seed: int = 0) -> dict:
    keys = jax.random.split(jax.random.key(seed), 8)
    return {
        "state": scatter_about(keys[0], (NV, NN, NN, NN, NXE, NYE, EZ), 0.1, 0.6, ((4, 8), (5, 32)), jnp.float32),
        "register": scatter_about(keys[1], (NV, NN, NN, NN, NXE, NYE, EZ), 1.0, 6.0, ((4, 8), (5, 32)), jnp.float32),
        "flux_x": scatter_about(keys[2], (NV, NV), NV ** -0.5, 2.5, (), jnp.float32),
        "flux_y": scatter_about(keys[3], (NV, NV), NV ** -0.5, 2.5, (), jnp.float32),
        "flux_z": scatter_about(keys[4], (NV, NV), NV ** -0.5, 2.5, (), jnp.float32),
        "viscosity": jnp.clip(jnp.exp(jax.random.uniform(keys[5], (NV,), jnp.float32, math.log(0.01), math.log(0.1))), 0.01, 0.1),
        "mortar_partner": draw_mortar_partner(jax.random.fold_in(keys[7], 71), 0),
    }


NODES = (-1.0, -0.7650553239294647, -0.2852315164806451, 0.2852315164806451, 0.7650553239294647, 1.0)
WEIGHTS = (1.0 / 15.0, 0.3784749562978470, 0.5548583770354863, 0.5548583770354863, 0.3784749562978470, 1.0 / 15.0)
end_weight = 1.0 / 15.0
step_size = 0.01
section_a = -0.4178904745
section_b = 1.5306374668
highest = lax.Precision.HIGHEST


def basis_tables():
    points = np.array(NODES)
    weights = np.array(WEIGHTS)
    count = points.shape[0]
    barycentric = np.array([1.0 / np.prod([points[first] - points[other] for other in range(count) if other != first]) for first in range(count)])
    derivative = np.zeros((count, count))
    for target in range(count):
        for source in range(count):
            if source != target:
                derivative[target, source] = barycentric[source] / barycentric[target] / (points[target] - points[source])
        derivative[target, target] = -np.sum(derivative[target])

    def lagrange(places):
        result = np.ones((count, count))
        for column in range(count):
            for other in range(count):
                if other != column:
                    result[:, column] *= (places - points[other]) / (points[column] - points[other])
        return result

    lower_map = lagrange((points - 1.0) / 2.0)
    upper_map = lagrange((points + 1.0) / 2.0)
    back_lower = 0.5 * lower_map.T * weights[None, :] / weights[:, None]
    back_upper = 0.5 * upper_map.T * weights[None, :] / weights[:, None]
    return tuple(jnp.asarray(table, dtype=jnp.float32) for table in (derivative, lower_map, upper_map, back_lower, back_upper))


def apply_nodes(matrix, source, axis):
    return jnp.moveaxis(jnp.tensordot(matrix, source, axes=((1,), (axis,)), precision=highest), 0, axis)


def mix_vars(matrix, source):
    return jnp.tensordot(matrix, source, axes=((1,), (0,)), precision=highest)


def add_ends(term, axis, first_add, last_add):
    head = [slice(None)] * term.ndim
    tail = [slice(None)] * term.ndim
    head[axis] = 0
    tail[axis] = term.shape[axis] - 1
    return term.at[tuple(head)].add(first_add).at[tuple(tail)].add(last_add)


def next_along(trace, axis, wrapping):
    if wrapping:
        return jnp.roll(trace, -1, axis)
    count = trace.shape[axis]
    blank = jnp.zeros_like(lax.slice_in_dim(trace, 0, 1, axis=axis))
    return jnp.concatenate([lax.slice_in_dim(trace, 1, count, axis=axis), blank], axis=axis)


def prev_along(trace, axis, wrapping):
    if wrapping:
        return jnp.roll(trace, 1, axis)
    count = trace.shape[axis]
    blank = jnp.zeros_like(lax.slice_in_dim(trace, 0, 1, axis=axis))
    return jnp.concatenate([blank, lax.slice_in_dim(trace, 0, count - 1, axis=axis)], axis=axis)


def face_traces(source, dimension):
    axis = 1 + dimension
    count = source.shape[axis]
    first = lax.index_in_dim(source, 0, axis, keepdims=False)
    last = lax.index_in_dim(source, count - 1, axis, keepdims=False)
    wrapping = dimension == 1
    outer_left = prev_along(last, 3 + dimension, wrapping)
    outer_right = next_along(first, 3 + dimension, wrapping)
    return first, last, outer_left, outer_right


def mortar_star(own_list, low_list, high_list, flux_fn, own_left, mortar_maps):
    lower_map, upper_map, back_lower, back_upper = mortar_maps
    own_low = [apply_nodes(lower_map, piece, 1) for piece in own_list]
    own_high = [apply_nodes(upper_map, piece, 1) for piece in own_list]
    far_low = [apply_nodes(upper_map, piece, 1) for piece in low_list]
    far_high = [apply_nodes(lower_map, piece, 1) for piece in high_list]

    def oriented(mine, theirs):
        if own_left:
            return flux_fn(mine, theirs)
        return flux_fn(theirs, mine)

    return apply_nodes(back_lower, oriented(own_low, far_low), 1) + apply_nodes(back_upper, oriented(own_high, far_high), 1)


def face_flux(matrix, speed, viscous, left_u, right_u, left_q, right_q):
    return mix_vars(matrix, 0.5 * (left_u + right_u)) - 0.5 * speed * (right_u - left_u) - viscous * (0.5 * (left_q + right_q))


def reference(state, register, flux_x, flux_y, flux_z, viscosity, mortar_partner):
    derivative, lower_map, upper_map, back_lower, back_upper = basis_tables()
    mortar_maps = (lower_map, upper_map, back_lower, back_upper)
    flux_mats = (flux_x, flux_y, flux_z)
    middle = state.shape[4] // 2
    total_y = state.shape[5]
    viscous_node = viscosity.reshape((-1, 1, 1, 1, 1, 1, 1))
    viscous_face = viscosity.reshape((-1, 1, 1, 1, 1, 1))
    viscous_mortar = viscosity.reshape((-1, 1, 1, 1, 1))
    rotor_first = mortar_partner[0].astype(jnp.int32)
    stator_first = mortar_partner[1].astype(jnp.int32)

    def partner_lists(first, last):
        rotor_face = last[:, :, :, middle - 1]
        stator_face = first[:, :, :, middle]
        rotor_low = jnp.take(stator_face, rotor_first, axis=3)
        rotor_high = jnp.take(stator_face, (rotor_first + 1) % total_y, axis=3)
        stator_low = jnp.take(rotor_face, stator_first, axis=3)
        stator_high = jnp.take(rotor_face, (stator_first + 1) % total_y, axis=3)
        return rotor_face, stator_face, rotor_low, rotor_high, stator_low, stator_high

    def average(left_side, right_side):
        return 0.5 * (left_side[0] + right_side[0])

    gradients = []
    saved = []
    state_parts = None
    for dimension in range(3):
        axis = 1 + dimension
        first, last, outer_left, outer_right = face_traces(state, dimension)
        star_left = 0.5 * (outer_left + first)
        star_right = 0.5 * (last + outer_right)
        if dimension == 0:
            state_parts = partner_lists(first, last)
            rotor_star = mortar_star([state_parts[0]], [state_parts[2]], [state_parts[3]], average, True, mortar_maps)
            stator_star = mortar_star([state_parts[1]], [state_parts[4]], [state_parts[5]], average, False, mortar_maps)
            star_right = star_right.at[:, :, :, middle - 1].set(rotor_star)
            star_left = star_left.at[:, :, :, middle].set(stator_star)
        gradient = apply_nodes(derivative, state, axis)
        gradient = add_ends(gradient, axis, -(star_left - first) / end_weight, (star_right - last) / end_weight)
        gradients.append(gradient)
        saved.append((first, last, outer_left, outer_right))

    residual = jnp.zeros_like(state)
    for dimension in range(3):
        axis = 1 + dimension
        matrix = flux_mats[dimension]
        speed = jnp.max(jnp.sum(jnp.abs(matrix), axis=1))
        gradient = gradients[dimension]
        flux_total = mix_vars(matrix, state) - viscous_node * gradient
        residual = residual - apply_nodes(derivative, flux_total, axis)
        first, last, outer_left, outer_right = saved[dimension]
        grad_first, grad_last, grad_outer_left, grad_outer_right = face_traces(gradient, dimension)
        star_left = face_flux(matrix, speed, viscous_face, outer_left, first, grad_outer_left, grad_first)
        star_right = face_flux(matrix, speed, viscous_face, last, outer_right, grad_last, grad_outer_right)
        if dimension == 0:
            grad_parts = partner_lists(grad_first, grad_last)

            def mortar_flux(left_side, right_side):
                return face_flux(matrix, speed, viscous_mortar, left_side[0], right_side[0], left_side[1], right_side[1])

            rotor_star = mortar_star([state_parts[0], grad_parts[0]], [state_parts[2], grad_parts[2]], [state_parts[3], grad_parts[3]], mortar_flux, True, mortar_maps)
            stator_star = mortar_star([state_parts[1], grad_parts[1]], [state_parts[4], grad_parts[4]], [state_parts[5], grad_parts[5]], mortar_flux, False, mortar_maps)
            star_right = star_right.at[:, :, :, middle - 1].set(rotor_star)
            star_left = star_left.at[:, :, :, middle].set(stator_star)
        count = flux_total.shape[axis]
        flux_first = lax.index_in_dim(flux_total, 0, axis, keepdims=False)
        flux_last = lax.index_in_dim(flux_total, count - 1, axis, keepdims=False)
        residual = add_ends(residual, axis, (star_left - flux_first) / end_weight, -(star_right - flux_last) / end_weight)

    register_new = section_a * register + residual
    state_new = state + section_b * step_size * register_new
    return state_new, register_new
```

```python
import functools

import jax
import jax.numpy as jnp
import numpy as np
from jax import lax
from jax.experimental import pallas as pl
from jax.experimental.pallas import tpu as pltpu
from jax.sharding import PartitionSpec as P

NODES = (
    -1.0,
    -0.7650553239294647,
    -0.2852315164806451,
    0.2852315164806451,
    0.7650553239294647,
    1.0,
)
WEIGHTS = (
    1.0 / 15.0,
    0.378474956297847,
    0.5548583770354863,
    0.5548583770354863,
    0.378474956297847,
    1.0 / 15.0,
)
half_gain = 7.5
step_size = 0.01
section_a = -0.4178904745
section_b = 1.5306374668
MESH = pl.DeviceIdType.MESH

NV = 5
NN = 6
FACE = NN * NN
BODY = NN * FACE
BODY_PAD = 224
LANES = 128
WIDE = NV * LANES
MSG = 2 * FACE
HEAD = 40
BLOCK = HEAD + MSG
TAIL = 32
MORT_K = 304


def basis_tables():
    points = np.array(NODES)
    weights = np.array(WEIGHTS)
    count = points.shape[0]
    barycentric = np.array(
        [
            1.0
            / np.prod([points[first] - points[other] for other in range(count) if other != first])
            for first in range(count)
        ]
    )
    derivative = np.zeros((count, count))
    for target in range(count):
        for source in range(count):
            if source != target:
                derivative[target, source] = (
                    barycentric[source] / barycentric[target] / (points[target] - points[source])
                )
        derivative[target, target] = -np.sum(derivative[target])

    def lagrange(places):
        result = np.ones((count, count))
        for column in range(count):
            for other in range(count):
                if other != column:
                    result[:, column] *= (places - points[other]) / (points[column] - points[other])
        return result

    lower_map = lagrange((points - 1.0) / 2.0)
    upper_map = lagrange((points + 1.0) / 2.0)
    back_lower = 0.5 * lower_map.T * weights[None, :] / weights[:, None]
    back_upper = 0.5 * upper_map.T * weights[None, :] / weights[:, None]
    return derivative, lower_map, upper_map, back_lower, back_upper


def along(matrix, dimension):
    parts = [np.eye(NN)] * 3
    parts[dimension] = matrix
    return np.kron(np.kron(parts[0], parts[1]), parts[2])


def operators():
    derivative, lower_map, upper_map, back_lower, back_upper = basis_tables()
    eye = np.eye(NN)
    first, last = eye[:1], eye[-1:]

    body = np.zeros((4 * BODY, BODY_PAD))
    second = np.zeros((BODY, BODY))
    for d in range(3):
        own = derivative + half_gain * (first.T @ first - last.T @ last)
        twice = derivative @ own + half_gain * (
            first.T @ derivative[:1] - last.T @ derivative[-1:]
        )
        body[d * BODY : (d + 1) * BODY, :BODY] = along(own, d)
        second += along(twice, d)
    body[3 * BODY :, :BODY] = second

    face = np.zeros((6 * BLOCK, BODY_PAD))
    far = np.zeros((3, BODY_PAD, 2 * MSG))
    for d in range(3):
        for end in range(2):
            row = first if end == 0 else last
            slope = derivative[:1] if end == 0 else derivative[-1:]
            sign = 1.0 if end == 0 else -1.0
            at = (2 * d + end) * BLOCK
            trace = along(row, d)
            face[at : at + FACE, :BODY] = trace
            face[at + HEAD : at + HEAD + FACE, :BODY] = sign * half_gain * along(slope, d)
            face[at + HEAD + FACE : at + BLOCK, :BODY] = half_gain * trace
            to = end * MSG
            column = derivative[:, :1] if end == 0 else derivative[:, -1:]
            far[d, :BODY, to : to + FACE] = trace.T
            far[d, :BODY, to + FACE : to + MSG] = -sign * along(column, d)

    low = back_lower @ upper_map
    high = back_upper @ lower_map
    same = back_lower @ lower_map + back_upper @ upper_map
    less = same - 2.0 * eye

    def on_face(matrix):
        return np.kron(matrix, eye)

    mortar = np.zeros((80, MORT_K))
    b, c = slice(0, FACE), slice(FACE, MSG)

    def put(rows, at, matrix):
        mortar[rows, at : at + FACE] = on_face(matrix)

    put(b, 0, eye - same)
    put(b, FACE, half_gain * (less @ less - low @ high - high @ low))
    put(c, FACE, same - eye)
    put(b, MSG, low)
    put(b, MSG + FACE, half_gain * (less @ low - low @ less))
    put(c, MSG + FACE, low)
    put(b, 2 * MSG, high)
    put(b, 2 * MSG + FACE, half_gain * (less @ high - high @ less))
    put(c, 2 * MSG + FACE, high)
    skip = FACE - TAIL
    put(b, 3 * MSG + skip, -half_gain * (low @ low))
    put(b, 3 * MSG + HEAD + skip, -half_gain * (high @ high))
    return face, body, far, mortar


def halves(matrix):
    high = np.asarray(matrix, np.float32).astype(jnp.bfloat16)
    low = (matrix - high.astype(np.float64)).astype(np.float32).astype(jnp.bfloat16)
    return np.stack([high, low])


def split(value):
    high = value.astype(jnp.bfloat16)
    return high, (value - high.astype(jnp.float32)).astype(jnp.bfloat16)


def dot3(matrix, high, low):
    def dot(a, x):
        return jnp.dot(a, x, preferred_element_type=jnp.float32)

    return dot(matrix[0], high) + (dot(matrix[0], low) + dot(matrix[1], high))


def kernel(
    shift,
    counts,
    state,
    face_hbm,
    body_hbm,
    far_hbm,
    mortar_hbm,
    edge,
    flux_x,
    flux_y,
    flux_z,
    viscosity,
    out,
    face_op,
    body_op,
    far_op,
    mortar_op,
    high,
    low,
    traces,
    message,
    inbox,
    mortar_in,
    zbox,
    local,
    total,
    load_sem,
    send_sem,
    recv_sem,
):
    axial_count, sectors = counts
    half = axial_count // 2
    me = lax.axis_index("axial")
    place = lax.axis_index("sector")
    is_rotor = me == half - 1
    is_mortar = jnp.logical_or(me == half - 1, me == half)
    has_left = jnp.logical_and(me != 0, me != half)
    has_right = jnp.logical_and(me != axial_count - 1, me != half - 1)
    after = lax.rem(place + 1, sectors)
    before = lax.rem(place + sectors - 1, sectors)
    as_low = lax.rem(
        place + jnp.where(is_rotor, (shift + 1) % sectors, (sectors - shift) % sectors), sectors
    )
    as_high = lax.rem(
        place + jnp.where(is_rotor, shift % sectors, (2 * sectors - shift - 1) % sectors), sectors
    )
    other_row = jnp.where(is_rotor, half, half - 1)

    loads = [
        pltpu.make_async_copy(source, target, load_sem.at[k])
        for k, (source, target) in enumerate(
            ((face_hbm, face_op), (body_hbm, body_op), (far_hbm, far_op), (mortar_hbm, mortar_op))
        )
    ]
    for load in loads:
        load.start()

    barrier = pltpu.get_barrier_semaphore()

    def greet(row, column):
        pl.semaphore_signal(barrier, inc=1, device_id=(row, column), device_id_type=MESH)

    greet(me, after)
    greet(me, before)

    @pl.when(has_left)
    def _():
        greet(me - 1, place)

    @pl.when(has_right)
    def _():
        greet(me + 1, place)

    @pl.when(is_mortar)
    def _():
        greet(other_row, as_low)
        greet(other_row, as_high)

    for v in range(NV):
        whole = jnp.concatenate(
            [state[v], jnp.zeros((BODY_PAD - BODY, LANES), jnp.float32)], axis=0
        )
        upper, lower = split(whole)
        high[:, v * LANES : (v + 1) * LANES] = upper
        low[:, v * LANES : (v + 1) * LANES] = lower

    fluxes = (flux_x, flux_y, flux_z)
    speeds = []
    for flux in fluxes:
        sums = []
        for row in range(NV):
            entry = jnp.abs(flux[row, 0])
            for column in range(1, NV):
                entry = entry + jnp.abs(flux[row, column])
            sums.append(entry)
        speed = sums[0]
        for entry in sums[1:]:
            speed = jnp.maximum(speed, entry)
        speeds.append(speed)

    def columns(v):
        return slice(v * LANES, (v + 1) * LANES)

    loads[0].wait()

    def make_messages(d):
        rows = slice(2 * d * BLOCK, (2 * d + 2) * BLOCK)
        traces[rows, :] = dot3(face_op[:, rows, :], high[...], low[...])
        for end in range(2):
            at = (2 * d + end) * BLOCK
            gain = half_gain if end == 1 else -half_gain
            trace = [traces[at : at + HEAD, columns(w)] for w in range(NV)]
            for v in range(NV):
                mixed = (half_gain * speeds[d]) * trace[v]
                for w in range(NV):
                    mixed = mixed + (gain * fluxes[d][v, w]) * trace[w]
                part = viscosity[v] * traces[at + HEAD : at + BLOCK, columns(v)]
                message[2 * d + end, :HEAD, columns(v)] = part[:HEAD] + mixed
                message[2 * d + end, HEAD:, columns(v)] = part[HEAD:]

    def closed(at, v):
        return jnp.concatenate(
            [
                (half_gain * half_gain * viscosity[v]) * traces[at : at + HEAD, columns(v)],
                jnp.zeros((MSG - HEAD, LANES), jnp.float32),
            ],
            axis=0,
        )

    def remote(source, target, k, row, column):
        return pltpu.make_async_remote_copy(
            src_ref=source,
            dst_ref=target,
            send_sem=send_sem.at[k],
            recv_sem=recv_sem.at[k],
            device_id=(row, column),
            device_id_type=MESH,
        )

    from_left = inbox.at[0:MSG]
    from_right = inbox.at[MSG : 2 * MSG]
    from_before = inbox.at[2 * MSG : 3 * MSG]
    from_after = inbox.at[3 * MSG : 4 * MSG]
    own = jnp.where(is_rotor, 1, 0)
    go_right = remote(message.at[1], from_left, 0, me + 1, place)
    go_left = remote(message.at[0], from_right, 1, me - 1, place)
    go_after = remote(message.at[3], from_before, 2, me, after)
    go_before = remote(message.at[2], from_after, 3, me, before)
    go_low = remote(message.at[own], mortar_in.at[MSG : 2 * MSG], 4, other_row, as_low)
    go_high = remote(message.at[own], mortar_in.at[2 * MSG : 3 * MSG], 5, other_row, as_high)
    tail = message.at[own, TAIL:]
    row_after = remote(tail, mortar_in.at[3 * MSG : 3 * MSG + HEAD], 6, me, after)
    row_before = remote(
        tail, mortar_in.at[3 * MSG + HEAD : 3 * MSG + 2 * HEAD], 7, me, before
    )

    make_messages(0)
    waits = jnp.where(is_mortar, 5, jnp.where(jnp.logical_or(me == 0, me == axial_count - 1), 3, 4))
    pl.semaphore_wait(barrier, waits)

    @pl.when(is_mortar)
    def _():
        go_low.start()
        go_high.start()
        row_after.start()
        row_before.start()

    @pl.when(has_right)
    def _():
        go_right.start()

    @pl.when(has_left)
    def _():
        go_left.start()

    make_messages(1)
    go_after.start()
    go_before.start()

    @pl.when(me == 0)
    def _():
        for v in range(NV):
            inbox[0:MSG, columns(v)] = closed(0, v)

    @pl.when(me == axial_count - 1)
    def _():
        for v in range(NV):
            inbox[MSG : 2 * MSG, columns(v)] = closed(BLOCK, v)

    make_messages(2)
    lane = lax.broadcasted_iota(jnp.int32, (MSG, LANES), 1)
    for v in range(NV):
        zbox[0:MSG, columns(v)] = jnp.where(
            lane == 0, closed(4 * BLOCK, v), pltpu.roll(message[5, :, columns(v)], 1, 1)
        )
        zbox[MSG:, columns(v)] = jnp.where(
            lane == LANES - 1,
            closed(5 * BLOCK, v),
            pltpu.roll(message[4, :, columns(v)], LANES - 1, 1),
        )

    loads[1].wait()
    local[...] = dot3(body_op, high[...], low[...])
    loads[2].wait()
    z_high, z_low = split(zbox[...])
    total[...] = dot3(far_op[2], z_high, z_low)[:BODY]

    for d in range(3):
        edge_gain = -half_gain * speeds[d]
        for v in range(NV):
            mixed = total[:, columns(v)] + (edge_gain * edge[d]) * state[v]
            if d == 0:
                mixed = mixed + viscosity[v] * local[3 * BODY :, columns(v)]
            for w in range(NV):
                mixed = mixed - fluxes[d][v, w] * local[d * BODY : (d + 1) * BODY, columns(w)]
            total[:, columns(v)] = mixed

    go_after.wait()
    go_before.wait()
    y_high, y_low = split(inbox[2 * MSG :])
    total[...] += dot3(far_op[1], y_high, y_low)[:BODY]

    loads[3].wait()

    @pl.when(has_right)
    def _():
        go_right.wait_send()
        go_left_in = remote(message.at[0], from_right, 1, me + 1, place)
        go_left_in.wait_recv()

    @pl.when(has_left)
    def _():
        go_left.wait_send()
        go_right_in = remote(message.at[1], from_left, 0, me - 1, place)
        go_right_in.wait_recv()

    @pl.when(is_mortar)
    def _():
        mortar_in[0:MSG] = message[own]
        mortar_in[3 * MSG + 2 * HEAD :] = jnp.zeros((MORT_K - 3 * MSG - 2 * HEAD, WIDE), jnp.float32)
        go_low.wait()
        go_high.wait()
        row_after.wait()
        row_before.wait()
        m_high, m_low = split(mortar_in[...])
        stand_in = dot3(mortar_op, m_high, m_low)[:MSG]
        slot = pl.multiple_of(own * MSG, 8)
        inbox[pl.ds(slot, MSG)] = stand_in

    x_high, x_low = split(inbox[: 2 * MSG])
    added = dot3(far_op[0], x_high, x_low)[:BODY]
    for v in range(NV):
        out[v] = total[:, columns(v)] + added[:, columns(v)]


def on_device(counts, tables, state, register, flux_x, flux_y, flux_z, viscosity, mortar_partner):
    axial_count, sectors = counts
    face, body, far, mortar, edge = tables
    flat = state.reshape((NV, BODY, LANES))
    shift = lax.rem(mortar_partner[0, 0] - lax.axis_index("sector") + sectors, sectors)
    vmem = pl.BlockSpec(memory_space=pltpu.VMEM)
    smem = pl.BlockSpec(memory_space=pltpu.SMEM)
    anywhere = pl.BlockSpec(memory_space=pl.ANY)

    def run(which):
        return pl.pallas_call(
            functools.partial(kernel, which, counts),
            out_shape=jax.ShapeDtypeStruct((NV, BODY, LANES), jnp.float32),
            in_specs=[vmem] + [anywhere] * 4 + [vmem] + [smem] * 4,
            out_specs=vmem,
            scratch_shapes=[
                pltpu.VMEM(face.shape, jnp.bfloat16),
                pltpu.VMEM(body.shape, jnp.bfloat16),
                pltpu.VMEM(far.shape, jnp.bfloat16),
                pltpu.VMEM(mortar.shape, jnp.bfloat16),
                pltpu.VMEM((BODY_PAD, WIDE), jnp.bfloat16),
                pltpu.VMEM((BODY_PAD, WIDE), jnp.bfloat16),
                pltpu.VMEM((6 * BLOCK, WIDE), jnp.float32),
                pltpu.VMEM((6, MSG, WIDE), jnp.float32),
                pltpu.VMEM((4 * MSG, WIDE), jnp.float32),
                pltpu.VMEM((MORT_K, WIDE), jnp.float32),
                pltpu.VMEM((2 * MSG, WIDE), jnp.float32),
                pltpu.VMEM((4 * BODY, WIDE), jnp.float32),
                pltpu.VMEM((BODY, WIDE), jnp.float32),
                pltpu.SemaphoreType.DMA((4,)),
                pltpu.SemaphoreType.DMA((8,)),
                pltpu.SemaphoreType.DMA((8,)),
            ],
            compiler_params=pltpu.CompilerParams(
                collective_id=which, has_side_effects=True, vmem_limit_bytes=40 * 1024 * 1024
            ),
            name=f"section_{which}",
        )

    operands = (flat, face, body, far, mortar, edge, flux_x, flux_y, flux_z, viscosity)
    residual = lax.switch(shift, [run(which) for which in range(BRANCHES or sectors)], *operands)
    residual = residual.reshape(state.shape)
    register_new = section_a * register + residual
    state_new = state + section_b * step_size * register_new
    return (state_new, register_new)


BRANCHES = 0


def solution(mesh):
    counts = (mesh.shape["axial"], mesh.shape["sector"])
    face, body, far, mortar = operators()
    edge = np.zeros((3, BODY, LANES), np.float32)
    ends = np.zeros(NN)
    ends[0] = ends[-1] = 1.0
    for d in range(3):
        edge[d] = np.diag(along(np.diag(ends), d))[:, None]
    far_halves = np.stack([halves(far[d]) for d in range(3)])
    tables = tuple(
        jnp.asarray(table)
        for table in (halves(face), halves(body), far_halves, halves(mortar), edge)
    )
    spec = P(None, None, None, None, "axial", "sector", None)
    return jax.shard_map(
        functools.partial(on_device, counts, tables),
        mesh=mesh,
        in_specs=(spec, spec, P(), P(), P(), P(), P(None, "sector")),
        out_specs=(spec, spec),
        check_vma=False,
    )
```

```python
import functools

import jax
import jax.numpy as jnp
import numpy as np
from jax import lax
from jax.experimental import pallas as pl
from jax.experimental.pallas import tpu as pltpu
from jax.sharding import PartitionSpec as P

NODES = (
    -1.0,
    -0.7650553239294647,
    -0.2852315164806451,
    0.2852315164806451,
    0.7650553239294647,
    1.0,
)
WEIGHTS = (
    1.0 / 15.0,
    0.378474956297847,
    0.5548583770354863,
    0.5548583770354863,
    0.378474956297847,
    1.0 / 15.0,
)
half_gain = 7.5
step_size = 0.01
section_a = -0.4178904745
section_b = 1.5306374668
MESH = pl.DeviceIdType.MESH

NV = 5
NN = 6
FACE = NN * NN
BODY = NN * FACE
BODY_PAD = 224
LANES = 128
WIDE = NV * LANES
MSG = 2 * FACE
HEAD = 40
BLOCK = HEAD + MSG
TAIL = 32
MORT_K = 304


def basis_tables():
    points = np.array(NODES)
    weights = np.array(WEIGHTS)
    count = points.shape[0]
    barycentric = np.array(
        [
            1.0
            / np.prod([points[first] - points[other] for other in range(count) if other != first])
            for first in range(count)
        ]
    )
    derivative = np.zeros((count, count))
    for target in range(count):
        for source in range(count):
            if source != target:
                derivative[target, source] = (
                    barycentric[source] / barycentric[target] / (points[target] - points[source])
                )
        derivative[target, target] = -np.sum(derivative[target])

    def lagrange(places):
        result = np.ones((count, count))
        for column in range(count):
            for other in range(count):
                if other != column:
                    result[:, column] *= (places - points[other]) / (points[column] - points[other])
        return result

    lower_map = lagrange((points - 1.0) / 2.0)
    upper_map = lagrange((points + 1.0) / 2.0)
    back_lower = 0.5 * lower_map.T * weights[None, :] / weights[:, None]
    back_upper = 0.5 * upper_map.T * weights[None, :] / weights[:, None]
    return derivative, lower_map, upper_map, back_lower, back_upper


def along(matrix, dimension):
    parts = [np.eye(NN)] * 3
    parts[dimension] = matrix
    return np.kron(np.kron(parts[0], parts[1]), parts[2])


def operators():
    derivative, lower_map, upper_map, back_lower, back_upper = basis_tables()
    eye = np.eye(NN)
    first, last = eye[:1], eye[-1:]

    body = np.zeros((4 * BODY, BODY_PAD))
    second = np.zeros((BODY, BODY))
    for d in range(3):
        own = derivative + half_gain * (first.T @ first - last.T @ last)
        twice = derivative @ own + half_gain * (
            first.T @ derivative[:1] - last.T @ derivative[-1:]
        )
        body[d * BODY : (d + 1) * BODY, :BODY] = along(own, d)
        second += along(twice, d)
    body[3 * BODY :, :BODY] = second

    face = np.zeros((6 * BLOCK, BODY_PAD))
    far = np.zeros((3, BODY_PAD, 2 * MSG))
    for d in range(3):
        for end in range(2):
            row = first if end == 0 else last
            slope = derivative[:1] if end == 0 else derivative[-1:]
            sign = 1.0 if end == 0 else -1.0
            at = (2 * d + end) * BLOCK
            trace = along(row, d)
            face[at : at + FACE, :BODY] = trace
            face[at + HEAD : at + HEAD + FACE, :BODY] = sign * half_gain * along(slope, d)
            face[at + HEAD + FACE : at + BLOCK, :BODY] = half_gain * trace
            to = end * MSG
            column = derivative[:, :1] if end == 0 else derivative[:, -1:]
            far[d, :BODY, to : to + FACE] = trace.T
            far[d, :BODY, to + FACE : to + MSG] = -sign * along(column, d)

    low = back_lower @ upper_map
    high = back_upper @ lower_map
    same = back_lower @ lower_map + back_upper @ upper_map
    less = same - 2.0 * eye

    def on_face(matrix):
        return np.kron(matrix, eye)

    mortar = np.zeros((80, MORT_K))
    b, c = slice(0, FACE), slice(FACE, MSG)

    def put(rows, at, matrix):
        mortar[rows, at : at + FACE] = on_face(matrix)

    put(b, 0, eye - same)
    put(b, FACE, half_gain * (less @ less - low @ high - high @ low))
    put(c, FACE, same - eye)
    put(b, MSG, low)
    put(b, MSG + FACE, half_gain * (less @ low - low @ less))
    put(c, MSG + FACE, low)
    put(b, 2 * MSG, high)
    put(b, 2 * MSG + FACE, half_gain * (less @ high - high @ less))
    put(c, 2 * MSG + FACE, high)
    skip = FACE - TAIL
    put(b, 3 * MSG + skip, -half_gain * (low @ low))
    put(b, 3 * MSG + HEAD + skip, -half_gain * (high @ high))
    return face, body, far, mortar


def halves(matrix):
    high = np.asarray(matrix, np.float32).astype(jnp.bfloat16)
    low = (matrix - high.astype(np.float64)).astype(np.float32).astype(jnp.bfloat16)
    return np.stack([high, low])


def split(value):
    high = value.astype(jnp.bfloat16)
    return high, (value - high.astype(jnp.float32)).astype(jnp.bfloat16)


def dot3(matrix, high, low):
    def dot(a, x):
        return jnp.dot(a, x, preferred_element_type=jnp.float32)

    upper, lower = matrix[0], matrix[1]
    return dot(upper, high) + (dot(upper, low) + dot(lower, high))


def place_of(counts):
    axial_count = counts[0]
    half = axial_count // 2
    me = lax.axis_index("axial")
    is_rotor = me == half - 1
    is_mortar = jnp.logical_or(me == half - 1, me == half)
    has_left = jnp.logical_and(me != 0, me != half)
    has_right = jnp.logical_and(me != axial_count - 1, me != half - 1)
    return me, is_rotor, is_mortar, has_left, has_right


def columns(v):
    return slice(v * LANES, (v + 1) * LANES)


def split_state(state, high, low):
    for v in range(NV):
        whole = jnp.concatenate(
            [state[v], jnp.zeros((BODY_PAD - BODY, LANES), jnp.float32)], axis=0
        )
        upper, lower = split(whole)
        high[:, columns(v)] = upper
        low[:, columns(v)] = lower


def speed_of(flux):
    sums = []
    for row in range(NV):
        entry = jnp.abs(flux[row, 0])
        for column in range(1, NV):
            entry = entry + jnp.abs(flux[row, column])
        sums.append(entry)
    speed = sums[0]
    for entry in sums[1:]:
        speed = jnp.maximum(speed, entry)
    return speed


def make_messages(d, first_row, flux, viscosity, face_op, high, low, traces, message):
    rows = slice(first_row, first_row + 2 * BLOCK)
    traces[rows, :] = dot3(face_op, high[...], low[...])
    speed = speed_of(flux)
    for end in range(2):
        at = first_row + end * BLOCK
        gain = half_gain if end == 1 else -half_gain
        trace = [traces[at : at + HEAD, columns(w)] for w in range(NV)]
        for v in range(NV):
            mixed = (half_gain * speed) * trace[v]
            for w in range(NV):
                mixed = mixed + (gain * flux[v, w]) * trace[w]
            part = viscosity[v] * traces[at + HEAD : at + BLOCK, columns(v)]
            message[2 * d + end, :HEAD, columns(v)] = part[:HEAD] + mixed
            message[2 * d + end, HEAD:, columns(v)] = part[HEAD:]


def closed(traces, viscosity, at, v):
    return jnp.concatenate(
        [
            (half_gain * half_gain * viscosity[v]) * traces[at : at + HEAD, columns(v)],
            jnp.zeros((MSG - HEAD, LANES), jnp.float32),
        ],
        axis=0,
    )


def pack(
    counts,
    state_hbm,
    face_hbm,
    flux_x_hbm,
    flux_y_hbm,
    viscosity_hbm,
    message_hbm,
    state,
    face_op,
    flux_x,
    flux_y,
    viscosity,
    message,
    high,
    low,
    traces,
    load_sem,
    store_sem,
):
    loads = [
        pltpu.make_async_copy(state_hbm, state, load_sem.at[0]),
        pltpu.make_async_copy(face_hbm.at[0], face_op.at[0], load_sem.at[1]),
        pltpu.make_async_copy(flux_x_hbm, flux_x, load_sem.at[2]),
        pltpu.make_async_copy(viscosity_hbm, viscosity, load_sem.at[3]),
        pltpu.make_async_copy(face_hbm.at[1], face_op.at[1], load_sem.at[4]),
        pltpu.make_async_copy(flux_y_hbm, flux_y, load_sem.at[5]),
    ]
    for load in loads:
        load.start()
    stores = [
        pltpu.make_async_copy(message.at[0:2], message_hbm.at[0:2], store_sem.at[0]),
        pltpu.make_async_copy(message.at[2:4], message_hbm.at[2:4], store_sem.at[1]),
    ]
    end_store = pltpu.make_async_copy(message.at[4], message_hbm.at[4], store_sem.at[2])
    me = lax.axis_index("axial")
    is_end = jnp.logical_or(me == 0, me == counts[0] - 1)

    loads[0].wait()
    split_state(state, high, low)
    for load in loads[1:4]:
        load.wait()
    make_messages(0, 0, flux_x, viscosity, face_op.at[0], high, low, traces, message)
    stores[0].start()
    loads[4].wait()
    loads[5].wait()
    make_messages(1, 2 * BLOCK, flux_y, viscosity, face_op.at[1], high, low, traces, message)
    stores[1].start()

    @pl.when(is_end)
    def _():
        at = pl.multiple_of(jnp.where(me == 0, 0, BLOCK), 8)
        for v in range(NV):
            message[4, :HEAD, columns(v)] = (
                half_gain * half_gain * viscosity[v]
            ) * traces[pl.ds(at, HEAD), columns(v)]
            message[4, HEAD:, columns(v)] = jnp.zeros((MSG - HEAD, LANES), jnp.float32)
        end_store.start()
        end_store.wait()

    for store in stores:
        store.wait()


def exchange(shift, counts, message, inbox, mortar_in, local_sem, send_sem, recv_sem):
    axial_count, sectors = counts
    half = axial_count // 2
    me, is_rotor, is_mortar, has_left, has_right = place_of(counts)
    is_end = jnp.logical_or(me == 0, me == axial_count - 1)
    place = lax.axis_index("sector")
    after = lax.rem(place + 1, sectors)
    before = lax.rem(place + sectors - 1, sectors)
    even = shift % 2 == 0
    turn = shift if even else shift + 1
    across = lax.rem(
        place + jnp.where(is_rotor, turn % sectors, (sectors - turn) % sectors), sectors
    )
    other_row = jnp.where(is_rotor, half, half - 1)
    own = jnp.where(is_rotor, 1, 0)

    barrier = pltpu.get_barrier_semaphore()

    def greet(row, column):
        pl.semaphore_signal(barrier, inc=1, device_id=(row, column), device_id_type=MESH)

    greet(me, after)
    greet(me, before)

    @pl.when(has_left)
    def _():
        greet(me - 1, place)

    @pl.when(has_right)
    def _():
        greet(me + 1, place)

    @pl.when(is_mortar)
    def _():
        greet(other_row, across)

    def remote(origin, target, k, row, column):
        return pltpu.make_async_remote_copy(
            src_ref=origin,
            dst_ref=target,
            send_sem=send_sem.at[k],
            recv_sem=recv_sem.at[k],
            device_id=(row, column),
            device_id_type=MESH,
        )

    from_left = inbox.at[0:MSG]
    from_right = inbox.at[MSG : 2 * MSG]
    from_before = inbox.at[2 * MSG : 3 * MSG]
    from_after = inbox.at[3 * MSG : 4 * MSG]
    go_right = remote(message.at[1], from_left, 0, me + 1, place)
    go_left = remote(message.at[0], from_right, 1, me - 1, place)
    go_after = remote(message.at[3], from_before, 2, me, after)
    go_before = remote(message.at[2], from_after, 3, me, before)
    tail = message.at[own, TAIL:]
    row_after = remote(tail, mortar_in.at[3 * MSG : 3 * MSG + HEAD], 4, me, after)
    row_before = remote(
        tail, mortar_in.at[3 * MSG + HEAD : 3 * MSG + 2 * HEAD], 5, me, before
    )

    def straight(rotor):
        slot = 1 if rotor == even else 2
        pieces = []
        for k, (start, stop) in enumerate(((0, HEAD), (HEAD, MSG))):
            there = 2 if slot == 1 else 1
            come = remote(
                message.at[1 if rotor else 0, start:stop],
                mortar_in.at[there * MSG + start : there * MSG + stop],
                6 + k,
                other_row,
                across,
            )
            wait = remote(
                message.at[1 if rotor else 0, start:stop],
                mortar_in.at[slot * MSG + start : slot * MSG + stop],
                6 + k,
                other_row,
                across,
            )
            hand = remote(
                mortar_in.at[slot * MSG + start : slot * MSG + stop],
                mortar_in.at[there * MSG + start : there * MSG + stop],
                8 + k,
                me,
                before if slot == 1 else after,
            )
            pieces.append((come, wait, hand))
        return pieces


    keep = pltpu.make_async_copy(message.at[own], mortar_in.at[0:MSG], local_sem.at[0])
    close = pltpu.make_async_copy(message.at[4], inbox.at[0:MSG], local_sem.at[1])
    close_last = pltpu.make_async_copy(message.at[4], inbox.at[MSG : 2 * MSG], local_sem.at[1])
    pl.semaphore_wait(barrier, jnp.where(is_mortar, 4, jnp.where(is_end, 3, 4)))

    for rotor in (True, False):

        @pl.when(me == (half - 1 if rotor else half))
        def _(rotor=rotor):
            for come, _, _ in straight(rotor):
                come.start()
            row_after.start()
            row_before.start()
            keep.start()

    go_after.start()
    go_before.start()

    @pl.when(has_right)
    def _():
        go_right.start()

    @pl.when(has_left)
    def _():
        go_left.start()

    @pl.when(me == 0)
    def _():
        close.start()

    @pl.when(me == axial_count - 1)
    def _():
        close_last.start()

    for rotor in (True, False):

        @pl.when(me == (half - 1 if rotor else half))
        def _(rotor=rotor):
            pieces = straight(rotor)
            for _, wait, hand in pieces:
                wait.wait_recv()
                hand.start()
            for come, _, hand in pieces:
                come.wait_send()
                hand.wait()
            row_after.wait()
            row_before.wait()
            keep.wait()

    go_after.wait()
    go_before.wait()

    @pl.when(has_right)
    def _():
        go_right.wait_send()
        remote(message.at[0], from_right, 1, me + 1, place).wait_recv()

    @pl.when(has_left)
    def _():
        go_left.wait_send()
        remote(message.at[1], from_left, 0, me - 1, place).wait_recv()

    @pl.when(me == 0)
    def _():
        close.wait()

    @pl.when(me == axial_count - 1)
    def _():
        close_last.wait()


def finish(
    counts,
    state,
    register,
    inbox_hbm,
    mortar_hbm,
    body_op,
    far_op,
    mortar_op,
    edge,
    face_op,
    flux_x,
    flux_y,
    flux_z,
    viscosity,
    state_new,
    register_new,
    inbox,
    mortar_in,
    high,
    low,
    traces,
    message,
    zbox,
    local,
    total,
    load_sem,
):
    me, is_rotor, is_mortar, has_left, has_right = place_of(counts)
    own = jnp.where(is_rotor, 1, 0)
    load_inbox = pltpu.make_async_copy(inbox_hbm, inbox, load_sem.at[0])
    load_mortar = pltpu.make_async_copy(mortar_hbm, mortar_in, load_sem.at[1])

    @pl.when(is_mortar)
    def _():
        load_mortar.start()

    load_inbox.start()
    fluxes = (flux_x, flux_y, flux_z)
    speeds = [speed_of(flux) for flux in fluxes]
    split_state(state, high, low)

    make_messages(0, 0, flux_z, viscosity, face_op, high, low, traces, message)
    lane = lax.broadcasted_iota(jnp.int32, (MSG, LANES), 1)
    for v in range(NV):
        zbox[0:MSG, columns(v)] = jnp.where(
            lane == 0,
            closed(traces, viscosity, 0, v),
            pltpu.roll(message[1, :, columns(v)], 1, 1),
        )
        zbox[MSG:, columns(v)] = jnp.where(
            lane == LANES - 1,
            closed(traces, viscosity, BLOCK, v),
            pltpu.roll(message[0, :, columns(v)], LANES - 1, 1),
        )

    local[...] = dot3(body_op, high[...], low[...])
    z_high, z_low = split(zbox[...])
    total[...] = dot3(far_op.at[2], z_high, z_low)[:BODY]

    for d in range(3):
        edge_gain = -half_gain * speeds[d]
        for v in range(NV):
            mixed = total[:, columns(v)] + (edge_gain * edge[d]) * state[v]
            if d == 0:
                mixed = mixed + viscosity[v] * local[3 * BODY :, columns(v)]
            for w in range(NV):
                mixed = mixed - fluxes[d][v, w] * local[d * BODY : (d + 1) * BODY, columns(w)]
            total[:, columns(v)] = mixed

    load_inbox.wait()
    y_high, y_low = split(inbox[2 * MSG :])
    total[...] += dot3(far_op.at[1], y_high, y_low)[:BODY]

    @pl.when(is_mortar)
    def _():
        load_mortar.wait()
        mortar_in[3 * MSG + 2 * HEAD :] = jnp.zeros((MORT_K - 3 * MSG - 2 * HEAD, WIDE), jnp.float32)
        m_high, m_low = split(mortar_in[...])
        stand_in = dot3(mortar_op, m_high, m_low)[:MSG]
        slot = pl.multiple_of(own * MSG, 8)
        inbox[pl.ds(slot, MSG)] = stand_in

    x_high, x_low = split(inbox[: 2 * MSG])
    added = dot3(far_op.at[0], x_high, x_low)[:BODY]
    for v in range(NV):
        fresh = section_a * register[v] + (total[:, columns(v)] + added[:, columns(v)])
        register_new[v] = fresh
        state_new[v] = state[v] + (section_b * step_size) * fresh


def on_device(counts, tables, state, register, flux_x, flux_y, flux_z, viscosity, mortar_partner):
    axial_count, sectors = counts
    face, face_z, body, far, mortar, edge = tables
    flat = state.reshape((NV, BODY, LANES))
    flat_register = register.reshape((NV, BODY, LANES))
    shift = lax.rem(mortar_partner[0, 0] - lax.axis_index("sector") + sectors, sectors)
    vmem = pl.BlockSpec(memory_space=pltpu.VMEM)
    smem = pl.BlockSpec(memory_space=pltpu.SMEM)
    hbm = pl.BlockSpec(memory_space=pltpu.HBM)
    half_state = pltpu.VMEM((BODY_PAD, WIDE), jnp.bfloat16)
    limit = 48 * 1024 * 1024

    message = pl.pallas_call(
        functools.partial(pack, counts),
        out_shape=jax.ShapeDtypeStruct((5, MSG, WIDE), jnp.float32),
        in_specs=[hbm] * 5,
        out_specs=hbm,
        scratch_shapes=[
            pltpu.VMEM((NV, BODY, LANES), jnp.float32),
            pltpu.VMEM(face.shape, jnp.bfloat16),
            pltpu.SMEM((NV, NV), jnp.float32),
            pltpu.SMEM((NV, NV), jnp.float32),
            pltpu.SMEM((NV,), jnp.float32),
            pltpu.VMEM((5, MSG, WIDE), jnp.float32),
            half_state,
            half_state,
            pltpu.VMEM((4 * BLOCK, WIDE), jnp.float32),
            pltpu.SemaphoreType.DMA((6,)),
            pltpu.SemaphoreType.DMA((3,)),
        ],
        compiler_params=pltpu.CompilerParams(vmem_limit_bytes=62 * 1024 * 1024),
        name="pack",
    )(flat, face, flux_x, flux_y, viscosity)

    def run(which):
        return pl.pallas_call(
            functools.partial(exchange, which, counts),
            out_shape=(
                jax.ShapeDtypeStruct((4 * MSG, WIDE), jnp.float32),
                jax.ShapeDtypeStruct((MORT_K, WIDE), jnp.float32),
            ),
            in_specs=[hbm],
            out_specs=(hbm, hbm),
            scratch_shapes=[
                pltpu.SemaphoreType.DMA((2,)),
                pltpu.SemaphoreType.DMA((10,)),
                pltpu.SemaphoreType.DMA((10,)),
            ],
            compiler_params=pltpu.CompilerParams(collective_id=which, has_side_effects=True),
            name=f"exchange_{which}",
        )

    inbox, mortar_in = lax.switch(shift, [run(which) for which in range(sectors)], message)

    whole = jax.ShapeDtypeStruct((NV, BODY, LANES), jnp.float32)
    state_new, register_new = pl.pallas_call(
        functools.partial(finish, counts),
        out_shape=(whole, whole),
        in_specs=[vmem] * 2 + [hbm] * 2 + [vmem] * 5 + [smem] * 4,
        out_specs=(vmem, vmem),
        scratch_shapes=[
            pltpu.VMEM((4 * MSG, WIDE), jnp.float32),
            pltpu.VMEM((MORT_K, WIDE), jnp.float32),
            half_state,
            half_state,
            pltpu.VMEM((2 * BLOCK, WIDE), jnp.float32),
            pltpu.VMEM((2, MSG, WIDE), jnp.float32),
            pltpu.VMEM((2 * MSG, WIDE), jnp.float32),
            pltpu.VMEM((4 * BODY, WIDE), jnp.float32),
            pltpu.VMEM((BODY, WIDE), jnp.float32),
            pltpu.SemaphoreType.DMA((2,)),
        ],
        compiler_params=pltpu.CompilerParams(vmem_limit_bytes=limit),
        name="finish",
    )(
        flat,
        flat_register,
        inbox,
        mortar_in,
        body,
        far,
        mortar,
        edge,
        face_z,
        flux_x,
        flux_y,
        flux_z,
        viscosity,
    )
    return (state_new.reshape(state.shape), register_new.reshape(state.shape))


def solution(mesh):
    counts = (mesh.shape["axial"], mesh.shape["sector"])
    face, body, far, mortar = operators()
    edge = np.zeros((3, BODY, LANES), np.float32)
    ends = np.zeros(NN)
    ends[0] = ends[-1] = 1.0
    for d in range(3):
        edge[d] = np.diag(along(np.diag(ends), d))[:, None]
    far_halves = np.stack([halves(far[d]) for d in range(3)])
    tables = tuple(
        jnp.asarray(table)
        for table in (
            np.stack([halves(face[: 2 * BLOCK]), halves(face[2 * BLOCK : 4 * BLOCK])]),
            halves(face[4 * BLOCK :]),
            halves(body),
            far_halves,
            halves(mortar),
            edge,
        )
    )
    spec = P(None, None, None, None, "axial", "sector", None)
    return jax.shard_map(
        functools.partial(on_device, counts, tables),
        mesh=mesh,
        in_specs=(spec, spec, P(), P(), P(), P(), P(None, "sector")),
        out_specs=(spec, spec),
        check_vma=False,
    )
```

```python
import functools

import jax
import jax.numpy as jnp
import numpy as np
from jax import lax
from jax.experimental import pallas as pl
from jax.experimental.pallas import tpu as pltpu
from jax.sharding import PartitionSpec as P

NODES = (
    -1.0,
    -0.7650553239294647,
    -0.2852315164806451,
    0.2852315164806451,
    0.7650553239294647,
    1.0,
)
WEIGHTS = (
    1.0 / 15.0,
    0.378474956297847,
    0.5548583770354863,
    0.5548583770354863,
    0.378474956297847,
    1.0 / 15.0,
)
half_gain = 7.5
step_size = 0.01
section_a = -0.4178904745
section_b = 1.5306374668
MESH = pl.DeviceIdType.MESH

NV = 5
NN = 6
FACE = NN * NN
BODY = NN * FACE
BODY_PAD = 224
LANES = 128
WIDE = NV * LANES
ROOM = WIDE + LANES
MSG = 2 * FACE
HEAD = 40
BLOCK = HEAD + MSG
TAIL = 32
MORT_K = 304
Z_FACE = 4 * BLOCK
OWN = 6 * BLOCK
TABLE = OWN + 4 * BODY
CHUNK = 512


def basis_tables():
    points = np.array(NODES)
    weights = np.array(WEIGHTS)
    count = points.shape[0]
    barycentric = np.array(
        [
            1.0
            / np.prod([points[first] - points[other] for other in range(count) if other != first])
            for first in range(count)
        ]
    )
    derivative = np.zeros((count, count))
    for target in range(count):
        for source in range(count):
            if source != target:
                derivative[target, source] = (
                    barycentric[source] / barycentric[target] / (points[target] - points[source])
                )
        derivative[target, target] = -np.sum(derivative[target])

    def lagrange(places):
        result = np.ones((count, count))
        for column in range(count):
            for other in range(count):
                if other != column:
                    result[:, column] *= (places - points[other]) / (points[column] - points[other])
        return result

    lower_map = lagrange((points - 1.0) / 2.0)
    upper_map = lagrange((points + 1.0) / 2.0)
    back_lower = 0.5 * lower_map.T * weights[None, :] / weights[:, None]
    back_upper = 0.5 * upper_map.T * weights[None, :] / weights[:, None]
    return derivative, lower_map, upper_map, back_lower, back_upper


def along(matrix, dimension):
    parts = [np.eye(NN)] * 3
    parts[dimension] = matrix
    return np.kron(np.kron(parts[0], parts[1]), parts[2])


def operators():
    derivative, lower_map, upper_map, back_lower, back_upper = basis_tables()
    eye = np.eye(NN)
    first, last = eye[:1], eye[-1:]

    body = np.zeros((4 * BODY, BODY_PAD))
    second = np.zeros((BODY, BODY))
    for d in range(3):
        own = derivative + half_gain * (first.T @ first - last.T @ last)
        twice = derivative @ own + half_gain * (
            first.T @ derivative[:1] - last.T @ derivative[-1:]
        )
        body[d * BODY : (d + 1) * BODY, :BODY] = along(own, d)
        second += along(twice, d)
    body[3 * BODY :, :BODY] = second

    face = np.zeros((6 * BLOCK, BODY_PAD))
    far = np.zeros((3, BODY_PAD, 2 * MSG))
    for d in range(3):
        for end in range(2):
            row = first if end == 0 else last
            slope = derivative[:1] if end == 0 else derivative[-1:]
            sign = 1.0 if end == 0 else -1.0
            at = (2 * d + end) * BLOCK
            trace = along(row, d)
            face[at : at + FACE, :BODY] = trace
            face[at + HEAD : at + HEAD + FACE, :BODY] = sign * half_gain * along(slope, d)
            face[at + HEAD + FACE : at + BLOCK, :BODY] = half_gain * trace
            to = end * MSG
            column = derivative[:, :1] if end == 0 else derivative[:, -1:]
            far[d, :BODY, to : to + FACE] = trace.T
            far[d, :BODY, to + FACE : to + MSG] = -sign * along(column, d)

    low = back_lower @ upper_map
    high = back_upper @ lower_map
    same = back_lower @ lower_map + back_upper @ upper_map
    less = same - 2.0 * eye

    def on_face(matrix):
        return np.kron(matrix, eye)

    mortar = np.zeros((80, MORT_K))
    b, c = slice(0, FACE), slice(FACE, MSG)

    def put(rows, at, matrix):
        mortar[rows, at : at + FACE] = on_face(matrix)

    put(b, 0, eye - same)
    put(b, FACE, half_gain * (less @ less - low @ high - high @ low))
    put(c, FACE, same - eye)
    put(b, MSG, low)
    put(b, MSG + FACE, half_gain * (less @ low - low @ less))
    put(c, MSG + FACE, low)
    put(b, 2 * MSG, high)
    put(b, 2 * MSG + FACE, half_gain * (less @ high - high @ less))
    put(c, 2 * MSG + FACE, high)
    skip = FACE - TAIL
    put(b, 3 * MSG + skip, -half_gain * (low @ low))
    put(b, 3 * MSG + HEAD + skip, -half_gain * (high @ high))
    return face, body, far, mortar


def thirds(matrix):
    high = np.asarray(matrix, np.float32).astype(jnp.bfloat16)
    low = (matrix - high.astype(np.float64)).astype(np.float32).astype(jnp.bfloat16)
    return np.concatenate([high, high, low], axis=-1)


def put_box(box, lanes, value):
    rows = value.shape[0]
    high = value.astype(jnp.bfloat16)
    box[0:rows, lanes] = high
    box[rows : 2 * rows, lanes] = (value - high.astype(jnp.float32)).astype(jnp.bfloat16)
    box[2 * rows : 3 * rows, lanes] = high


def place_of(counts):
    axial_count = counts[0]
    half = axial_count // 2
    me = lax.axis_index("axial")
    is_rotor = me == half - 1
    is_mortar = jnp.logical_or(me == half - 1, me == half)
    has_left = jnp.logical_and(me != 0, me != half)
    has_right = jnp.logical_and(me != axial_count - 1, me != half - 1)
    return me, is_rotor, is_mortar, has_left, has_right


def columns(v):
    return slice(v * LANES, (v + 1) * LANES)


def crowding(turn):
    hops = (1, 3, -3, -1)
    steps = [hops[(turn + core) // 2 % 4] for core in range(2)]
    return max(sum(h for h in steps if h > 0), -sum(h for h in steps if h < 0))


def exchange(
    shift,
    counts,
    state_hbm,
    body_hbm,
    far_hbm,
    mortar_hbm,
    edge_hbm,
    flux_x_hbm,
    flux_y_hbm,
    flux_z_hbm,
    viscosity_hbm,
    residual_hbm,
    state,
    body_op,
    far_op,
    mortar_op,
    edge,
    flux,
    viscosity,
    speed,
    message,
    box,
    inbox,
    mortar_in,
    mortar_box,
    stand_in,
    z_message,
    far_box,
    local,
    total,
    load_sem,
    local_sem,
    send_sem,
    recv_sem,
):
    axial_count, sectors = counts
    half = axial_count // 2
    me, is_rotor, is_mortar, has_left, has_right = place_of(counts)
    is_end = jnp.logical_or(me == 0, me == axial_count - 1)
    place = lax.axis_index("sector")
    after = lax.rem(place + 1, sectors)
    before = lax.rem(place + sectors - 1, sectors)
    turn = min((shift, shift + 1), key=crowding)
    across = lax.rem(
        place + jnp.where(is_rotor, turn % sectors, (sectors - turn) % sectors), sectors
    )
    other_row = jnp.where(is_rotor, half, half - 1)
    own = jnp.where(is_rotor, 1, 0)

    loads = [
        pltpu.make_async_copy(origin, target, load_sem.at[k])
        for k, (origin, target) in enumerate(
            (
                (state_hbm, state),
                (body_hbm.at[0:CHUNK], body_op.at[0:CHUNK]),
                (flux_x_hbm, flux.at[0]),
                (flux_y_hbm, flux.at[1]),
                (viscosity_hbm, viscosity),
                (flux_z_hbm, flux.at[2]),
                (body_hbm.at[CHUNK:], body_op.at[CHUNK:]),
                (far_hbm, far_op),
                (edge_hbm, edge),
                (mortar_hbm, mortar_op),
            )
        )
    ]
    for load in loads:
        load.start()

    barrier = pltpu.get_barrier_semaphore()

    def greet(row, column):
        pl.semaphore_signal(barrier, inc=1, device_id=(row, column), device_id_type=MESH)

    greet(me, after)
    greet(me, before)

    @pl.when(has_left)
    def _():
        greet(me - 1, place)

    @pl.when(has_right)
    def _():
        greet(me + 1, place)

    @pl.when(is_mortar)
    def _():
        greet(other_row, across)

    def remote(origin, target, k, row, column):
        return pltpu.make_async_remote_copy(
            src_ref=origin,
            dst_ref=target,
            send_sem=send_sem.at[k],
            recv_sem=recv_sem.at[k],
            device_id=(row, column),
            device_id_type=MESH,
        )

    from_left = inbox.at[0:MSG]
    from_right = inbox.at[MSG : 2 * MSG]
    from_before = inbox.at[2 * MSG : 3 * MSG]
    from_after = inbox.at[3 * MSG : 4 * MSG]
    go_right = remote(message.at[1], from_left, 0, me + 1, place)
    go_left = remote(message.at[0], from_right, 1, me - 1, place)
    go_after = remote(message.at[3], from_before, 2, me, after)
    go_before = remote(message.at[2], from_after, 3, me, before)
    tail = message.at[own, TAIL:]
    row_after = remote(tail, mortar_in.at[3 * MSG : 3 * MSG + HEAD], 4, me, after)
    row_before = remote(
        tail, mortar_in.at[3 * MSG + HEAD : 3 * MSG + 2 * HEAD], 5, me, before
    )

    low_first = jnp.where(is_rotor, 1, 0) == (1 if turn == shift else 0)
    slot = jnp.where(low_first, 1, 2) * MSG
    other = jnp.where(low_first, 2, 1) * MSG
    neighbour = jnp.where(low_first, before, after)
    pieces = []
    for k, (start, stop) in enumerate(((0, HEAD), (HEAD, MSG))):
        mine = message.at[own, start:stop]
        straight = mortar_in.at[pl.ds(pl.multiple_of(slot + start, 8), stop - start)]
        passed = mortar_in.at[pl.ds(pl.multiple_of(other + start, 8), stop - start)]
        pieces.append(
            (
                remote(mine, passed, 6 + k, other_row, across),
                remote(mine, straight, 6 + k, other_row, across),
                remote(straight, passed, 8 + k, me, neighbour),
            )
        )

    keep = pltpu.make_async_copy(message.at[own], mortar_in.at[0:MSG], local_sem.at[0])
    end_slot = pl.multiple_of(jnp.where(me == 0, 0, MSG), 8)
    close = pltpu.make_async_copy(message.at[4], inbox.at[pl.ds(end_slot, MSG)], local_sem.at[1])

    loads[0].wait()

    def pair(k):
        return pl.ds(pl.multiple_of(k * 2 * LANES, 2 * LANES), 2 * LANES)

    def one(v):
        return pl.ds(pl.multiple_of(v * LANES, LANES), LANES)

    pairs = (NV + 1) // 2

    def split_one(v, carry):
        whole = jnp.concatenate(
            [state[v], jnp.zeros((BODY_PAD - BODY, LANES), jnp.float32)], axis=0
        )
        put_box(box, one(v), whole)
        return carry

    lax.fori_loop(0, NV, split_one, 0)
    for load in loads[1:6]:
        load.wait()

    def find_speed(d, carry):
        largest = jnp.float32(0.0)
        for row in range(NV):
            entry = jnp.abs(flux[d, row, 0])
            for column in range(1, NV):
                entry = entry + jnp.abs(flux[d, row, column])
            largest = jnp.maximum(largest, entry)
        speed[d] = half_gain * largest
        return carry

    lax.fori_loop(0, 3, find_speed, 0)

    def make_message(origin, base, d, end, v, target, face):
        gain = jnp.where(end == 1, half_gain, -half_gain)
        at = pl.multiple_of(base, 8)
        lanes = one(v)
        mixed = speed[d] * origin[pl.ds(at, HEAD), lanes]
        for w in range(NV):
            mixed = mixed + (gain * flux[d, v, w]) * origin[pl.ds(at, HEAD), columns(w)]
        part = viscosity[v] * origin[pl.ds(pl.multiple_of(at + HEAD, 8), MSG), lanes]
        target[face, :HEAD, lanes] = part[:HEAD] + mixed
        target[face, HEAD:, lanes] = part[HEAD:]

    def make_outgoing(k, carry):
        face, v = k // NV, lax.rem(k, NV)
        make_message(local, face * BLOCK, face // 2, lax.rem(face, 2), v, message, face)
        return carry

    def send_messages():
        lax.fori_loop(0, 4 * NV, make_outgoing, 0)

        @pl.when(is_end)
        def _():
            at = pl.multiple_of(jnp.where(me == 0, 0, BLOCK), 8)

            def close_one(v, carry):
                lanes = pl.ds(pl.multiple_of(v * LANES, LANES), LANES)
                message[4, :HEAD, lanes] = (half_gain * half_gain * viscosity[v]) * local[
                    pl.ds(at, HEAD), lanes
                ]
                message[4, HEAD:, lanes] = jnp.zeros((MSG - HEAD, LANES), jnp.float32)
                return carry

            lax.fori_loop(0, NV, close_one, 0)

        pl.semaphore_wait(barrier, jnp.where(is_mortar, 4, jnp.where(is_end, 3, 4)))

        @pl.when(is_mortar)
        def _():
            for send, _, _ in pieces:
                send.start()
            row_after.start()
            row_before.start()
            keep.start()

        go_after.start()
        go_before.start()

        @pl.when(has_right)
        def _():
            go_right.start()

        @pl.when(has_left)
        def _():
            go_left.start()

        @pl.when(is_end)
        def _():
            close.start()

    def chunk_of(c, carry):
        rows = pl.ds(pl.multiple_of(c * CHUNK, 16), CHUNK)

        @pl.when(c == 1)
        def _():
            loads[6].wait()

        def local_pair(k, carry):
            lanes = pair(k)
            local[rows, lanes] = jnp.dot(
                body_op[rows, :], box[:, lanes], preferred_element_type=jnp.float32
            )
            return carry

        lax.fori_loop(0, pairs, local_pair, 0)

        @pl.when(c == 0)
        def _():
            send_messages()

        return carry

    lax.fori_loop(0, TABLE // CHUNK, chunk_of, 0)

    def make_inner(k, carry):
        end, v = k // NV, lax.rem(k, NV)
        make_message(local, Z_FACE + end * BLOCK, 2, end, v, z_message, end)
        return carry

    lax.fori_loop(0, 2 * NV, make_inner, 0)
    lane = lax.broadcasted_iota(jnp.int32, (MSG, LANES), 1)

    def fill_z(v, carry):
        lanes = one(v)
        closing = half_gain * half_gain * viscosity[v]
        blank = jnp.zeros((MSG - HEAD, LANES), jnp.float32)
        sides = []
        for end, (edge_lane, by) in enumerate(((0, 1), (LANES - 1, LANES - 1))):
            at = Z_FACE + end * BLOCK
            outside = jnp.concatenate([closing * local[at : at + HEAD, lanes], blank], axis=0)
            inside = pltpu.roll(z_message[1 - end, :, lanes], by, 1)
            sides.append(jnp.where(lane == edge_lane, outside, inside))
        put_box(far_box, lanes, jnp.concatenate(sides, axis=0))
        return carry

    loads[8].wait()
    rows_at_once = 24

    def mix_rows(k, carry):
        rows = pl.ds(pl.multiple_of(k * rows_at_once, 8), rows_at_once)
        weight = -speed[0] * edge[0, rows]
        for d in range(1, 3):
            weight = weight - speed[d] * edge[d, rows]

        def mix(v, carry):
            lanes = one(v)
            at = pl.ds(pl.multiple_of(OWN + 3 * BODY + k * rows_at_once, 8), rows_at_once)
            mixed = weight * state[v, rows] + viscosity[v] * local[at, lanes]
            for d in range(3):
                at = pl.ds(pl.multiple_of(OWN + d * BODY + k * rows_at_once, 8), rows_at_once)
                for w in range(NV):
                    mixed = mixed - flux[d, v, w] * local[at, columns(w)]
            total[rows, lanes] = mixed
            return carry

        return lax.fori_loop(0, NV, mix, carry)

    lax.fori_loop(0, BODY // rows_at_once, mix_rows, 0)

    loads[7].wait()
    loads[9].wait()

    def take_along():
        @pl.when(is_mortar)
        def _():
            for _, wait, hand in pieces:
                wait.wait_recv()
                hand.start()

        go_after.wait()
        go_before.wait()

    def take_axis():
        @pl.when(has_right)
        def _():
            go_right.wait_send()
            remote(message.at[0], from_right, 1, me + 1, place).wait_recv()

        @pl.when(has_left)
        def _():
            go_left.wait_send()
            remote(message.at[1], from_left, 0, me - 1, place).wait_recv()

        @pl.when(is_end)
        def _():
            close.wait()

        @pl.when(is_mortar)
        def _():
            for send, _, hand in pieces:
                send.wait_send()
                hand.wait()
            row_after.wait()
            row_before.wait()
            keep.wait()
            mortar_in[3 * MSG + 2 * HEAD :] = jnp.zeros(
                (MORT_K - 3 * MSG - 2 * HEAD, WIDE), jnp.float32
            )

            def fill_mortar(v, carry):
                put_box(mortar_box, one(v), mortar_in[:, one(v)])
                return carry

            lax.fori_loop(0, NV, fill_mortar, 0)

            def stand_pair(k, carry):
                lanes = pair(k)
                stand_in[:, lanes] = jnp.dot(
                    mortar_op[...], mortar_box[:, lanes], preferred_element_type=jnp.float32
                )
                return carry

            lax.fori_loop(0, pairs, stand_pair, 0)
            slot_rows = pl.ds(pl.multiple_of(own * MSG, 8), MSG)
            for v in range(NV):
                inbox[slot_rows, columns(v)] = stand_in[:MSG, columns(v)]

    def add_far(stage, carry):
        d = 2 - stage

        @pl.when(stage == 0)
        def _():
            lax.fori_loop(0, NV, fill_z, 0)

        @pl.when(stage == 1)
        def _():
            take_along()

        @pl.when(stage == 2)
        def _():
            take_axis()

        @pl.when(stage > 0)
        def _():
            first_row = pl.multiple_of(d * 2 * MSG, 8)

            def fill(v, carry):
                put_box(far_box, one(v), inbox[pl.ds(first_row, 2 * MSG), one(v)])
                return carry

            lax.fori_loop(0, NV, fill, 0)

        def add(k, carry):
            lanes = pair(k)
            term = jnp.dot(far_op[d], far_box[:, lanes], preferred_element_type=jnp.float32)
            total[:, lanes] += term[:BODY]
            return carry

        return lax.fori_loop(0, pairs, add, carry)

    lax.fori_loop(0, 3, add_far, 0)
    store = pltpu.make_async_copy(total.at[:, 0:WIDE], residual_hbm, local_sem.at[2])
    store.start()
    store.wait()


def finish(state, register, residual, state_new, register_new):
    for v in range(NV):
        fresh = section_a * register[v] + residual[:, columns(v)]
        register_new[v] = fresh
        state_new[v] = state[v] + (section_b * step_size) * fresh


def on_device(counts, tables, state, register, flux_x, flux_y, flux_z, viscosity, mortar_partner):
    axial_count, sectors = counts
    body, far, mortar, edge = tables
    flat = state.reshape((NV, BODY, LANES))
    flat_register = register.reshape((NV, BODY, LANES))
    vmem = pl.BlockSpec(memory_space=pltpu.VMEM)
    hbm = pl.BlockSpec(memory_space=pltpu.HBM)
    limit = 48 * 1024 * 1024

    shift = lax.rem(mortar_partner[0, 0] - lax.axis_index("sector") + sectors, sectors)

    def run(which):
        return pl.pallas_call(
            functools.partial(exchange, which, counts),
            out_shape=jax.ShapeDtypeStruct((BODY, WIDE), jnp.float32),
            in_specs=[hbm] * 9,
            out_specs=hbm,
            scratch_shapes=[
                pltpu.VMEM((NV, BODY, LANES), jnp.float32),
                pltpu.VMEM(body.shape, jnp.bfloat16),
                pltpu.VMEM(far.shape, jnp.bfloat16),
                pltpu.VMEM(mortar.shape, jnp.bfloat16),
                pltpu.VMEM(edge.shape, jnp.float32),
                pltpu.SMEM((3, NV, NV), jnp.float32),
                pltpu.SMEM((NV,), jnp.float32),
                pltpu.SMEM((3,), jnp.float32),
                pltpu.VMEM((5, MSG, WIDE), jnp.float32),
                pltpu.VMEM((3 * BODY_PAD, ROOM), jnp.bfloat16),
                pltpu.VMEM((4 * MSG, WIDE), jnp.float32),
                pltpu.VMEM((MORT_K, WIDE), jnp.float32),
                pltpu.VMEM((3 * MORT_K, ROOM), jnp.bfloat16),
                pltpu.VMEM((80, ROOM), jnp.float32),
                pltpu.VMEM((2, MSG, WIDE), jnp.float32),
                pltpu.VMEM((6 * MSG, ROOM), jnp.bfloat16),
                pltpu.VMEM((TABLE, ROOM), jnp.float32),
                pltpu.VMEM((BODY, ROOM), jnp.float32),
                pltpu.SemaphoreType.DMA((10,)),
                pltpu.SemaphoreType.DMA((3,)),
                pltpu.SemaphoreType.DMA((10,)),
                pltpu.SemaphoreType.DMA((10,)),
            ],
            compiler_params=pltpu.CompilerParams(
                collective_id=which, has_side_effects=True, vmem_limit_bytes=limit
            ),
            name=f"exchange_{which}",
        )

    residual = lax.switch(
        shift,
        [run(which) for which in range(sectors)],
        flat,
        body,
        far,
        mortar,
        edge,
        flux_x,
        flux_y,
        flux_z,
        viscosity,
    )

    whole = jax.ShapeDtypeStruct((NV, BODY, LANES), jnp.float32)
    state_new, register_new = pl.pallas_call(
        finish,
        out_shape=(whole, whole),
        in_specs=[vmem] * 3,
        out_specs=(vmem, vmem),
        name="finish",
    )(flat, flat_register, residual)
    return (state_new.reshape(state.shape), register_new.reshape(state.shape))


def solution(mesh):
    counts = (mesh.shape["axial"], mesh.shape["sector"])
    face, body, far, mortar = operators()
    edge = np.zeros((3, BODY, LANES), np.float32)
    ends = np.zeros(NN)
    ends[0] = ends[-1] = 1.0
    for d in range(3):
        edge[d] = np.diag(along(np.diag(ends), d))[:, None]
    tables = tuple(
        jnp.asarray(table)
        for table in (
            thirds(np.concatenate([face, body])),
            thirds(far),
            thirds(mortar),
            edge,
        )
    )
    spec = P(None, None, None, None, "axial", "sector", None)
    return jax.shard_map(
        functools.partial(on_device, counts, tables),
        mesh=mesh,
        in_specs=(spec, spec, P(), P(), P(), P(), P(None, "sector")),
        out_specs=(spec, spec),
        check_vma=False,
    )
```

```python
import functools

import jax
import jax.numpy as jnp
import numpy as np
from jax import lax
from jax.experimental import pallas as pl
from jax.experimental.pallas import tpu as pltpu
from jax.sharding import PartitionSpec as P

NODES = (
    -1.0,
    -0.7650553239294647,
    -0.2852315164806451,
    0.2852315164806451,
    0.7650553239294647,
    1.0,
)
WEIGHTS = (
    1.0 / 15.0,
    0.378474956297847,
    0.5548583770354863,
    0.5548583770354863,
    0.378474956297847,
    1.0 / 15.0,
)
half_gain = 7.5
step_size = 0.01
section_a = -0.4178904745
section_b = 1.5306374668
MESH = pl.DeviceIdType.MESH

NV = 5
NN = 6
FACE = NN * NN
BODY = NN * FACE
BODY_PAD = 224
LANES = 128
WIDE = NV * LANES
ROOM = WIDE + LANES
MSG = 2 * FACE
HEAD = 40
BLOCK = HEAD + MSG
TAIL = 32
MORT_K = 368
Z_FACE = 4 * BLOCK
OWN = 6 * BLOCK
TABLE = OWN + 4 * BODY
CHUNK = 256


def basis_tables():
    points = np.array(NODES)
    weights = np.array(WEIGHTS)
    count = points.shape[0]
    barycentric = np.array(
        [
            1.0
            / np.prod([points[first] - points[other] for other in range(count) if other != first])
            for first in range(count)
        ]
    )
    derivative = np.zeros((count, count))
    for target in range(count):
        for source in range(count):
            if source != target:
                derivative[target, source] = (
                    barycentric[source] / barycentric[target] / (points[target] - points[source])
                )
        derivative[target, target] = -np.sum(derivative[target])

    def lagrange(places):
        result = np.ones((count, count))
        for column in range(count):
            for other in range(count):
                if other != column:
                    result[:, column] *= (places - points[other]) / (points[column] - points[other])
        return result

    lower_map = lagrange((points - 1.0) / 2.0)
    upper_map = lagrange((points + 1.0) / 2.0)
    back_lower = 0.5 * lower_map.T * weights[None, :] / weights[:, None]
    back_upper = 0.5 * upper_map.T * weights[None, :] / weights[:, None]
    return derivative, lower_map, upper_map, back_lower, back_upper


def along(matrix, dimension):
    parts = [np.eye(NN)] * 3
    parts[dimension] = matrix
    return np.kron(np.kron(parts[0], parts[1]), parts[2])


def operators():
    derivative, lower_map, upper_map, back_lower, back_upper = basis_tables()
    eye = np.eye(NN)
    first, last = eye[:1], eye[-1:]

    body = np.zeros((4 * BODY, BODY_PAD))
    second = np.zeros((BODY, BODY))
    for d in range(3):
        own = derivative + half_gain * (first.T @ first - last.T @ last)
        twice = derivative @ own + half_gain * (
            first.T @ derivative[:1] - last.T @ derivative[-1:]
        )
        body[d * BODY : (d + 1) * BODY, :BODY] = along(own, d)
        second += along(twice, d)
    body[3 * BODY :, :BODY] = second

    face = np.zeros((6 * BLOCK, BODY_PAD))
    far = np.zeros((3, BODY_PAD, 2 * MSG))
    for d in range(3):
        for end in range(2):
            row = first if end == 0 else last
            slope = derivative[:1] if end == 0 else derivative[-1:]
            sign = 1.0 if end == 0 else -1.0
            at = (2 * d + end) * BLOCK
            trace = along(row, d)
            face[at : at + FACE, :BODY] = trace
            face[at + HEAD : at + HEAD + FACE, :BODY] = sign * half_gain * along(slope, d)
            face[at + HEAD + FACE : at + BLOCK, :BODY] = half_gain * trace
            to = end * MSG
            column = derivative[:, :1] if end == 0 else derivative[:, -1:]
            far[d, :BODY, to : to + FACE] = trace.T
            far[d, :BODY, to + FACE : to + MSG] = -sign * along(column, d)

    low = back_lower @ upper_map
    high = back_upper @ lower_map
    same = back_lower @ lower_map + back_upper @ upper_map
    less = same - 2.0 * eye

    def on_face(matrix):
        return np.kron(matrix, eye)

    mortar = np.zeros((2, 80, MORT_K))
    b, c = slice(0, FACE), slice(FACE, MSG)
    skip = FACE - TAIL
    for straight_low in range(2):

        def put(rows, at, matrix):
            mortar[straight_low, rows, at : at + FACE] = on_face(matrix)

        low_at, high_at = (MSG, 3 * MSG) if straight_low else (2 * MSG, MSG)
        put(b, 0, eye - same)
        put(b, FACE, half_gain * (less @ less - low @ high - high @ low))
        put(c, FACE, same - eye)
        for matrix, at in ((low, low_at), (high, high_at)):
            put(b, at, matrix)
            put(b, at + FACE, half_gain * (less @ matrix - matrix @ less))
            put(c, at + FACE, matrix)
        put(b, 4 * MSG + skip, -half_gain * (low @ low))
        put(b, 4 * MSG + HEAD + skip, -half_gain * (high @ high))
    return face, body, far, mortar


def thirds(matrix):
    high = np.asarray(matrix, np.float32).astype(jnp.bfloat16)
    low = (matrix - high.astype(np.float64)).astype(np.float32).astype(jnp.bfloat16)
    return np.concatenate([high, high, low], axis=-1)


def put_box(box, lanes, value):
    rows = value.shape[0]
    high = value.astype(jnp.bfloat16)
    box[0:rows, lanes] = high
    box[rows : 2 * rows, lanes] = (value - high.astype(jnp.float32)).astype(jnp.bfloat16)
    box[2 * rows : 3 * rows, lanes] = high


def place_of(counts):
    axial_count = counts[0]
    half = axial_count // 2
    me = lax.axis_index("axial")
    is_rotor = me == half - 1
    is_mortar = jnp.logical_or(me == half - 1, me == half)
    has_left = jnp.logical_and(me != 0, me != half)
    has_right = jnp.logical_and(me != axial_count - 1, me != half - 1)
    return me, is_rotor, is_mortar, has_left, has_right


def columns(v):
    return slice(v * LANES, (v + 1) * LANES)


def exchange(
    shift,
    counts,
    odd,
    state_hbm,
    body_hbm,
    far_hbm,
    mortar_hbm,
    edge_hbm,
    flux_x_hbm,
    flux_y_hbm,
    flux_z_hbm,
    viscosity_hbm,
    residual_hbm,
    state,
    body_op,
    far_op,
    mortar_op,
    edge,
    flux,
    viscosity,
    speed,
    message,
    box,
    inbox,
    mortar_in,
    mortar_box,
    stand_in,
    z_message,
    far_box,
    local,
    total,
    load_sem,
    local_sem,
    send_sem,
    recv_sem,
):
    axial_count, sectors = counts
    half = axial_count // 2
    me, is_rotor, is_mortar, has_left, has_right = place_of(counts)
    is_end = jnp.logical_or(me == 0, me == axial_count - 1)
    place = lax.axis_index("sector")
    after = lax.rem(place + 1, sectors)
    before = lax.rem(place + sectors - 1, sectors)
    turn = 2 * shift + 1
    across = lax.rem(
        place + jnp.where(is_rotor, turn % sectors, (sectors - turn) % sectors), sectors
    )
    other_row = jnp.where(is_rotor, half, half - 1)
    own = jnp.where(is_rotor, 1, 0)

    barrier = pltpu.get_barrier_semaphore()

    def greet(row, column):
        pl.semaphore_signal(barrier, inc=1, device_id=(row, column), device_id_type=MESH)

    @pl.when(is_mortar)
    def _():
        greet(other_row, across)

    greet(me, after)
    greet(me, before)

    @pl.when(has_left)
    def _():
        greet(me - 1, place)

    @pl.when(has_right)
    def _():
        greet(me + 1, place)

    loads = [
        pltpu.make_async_copy(origin, target, load_sem.at[k])
        for k, (origin, target) in enumerate(
            (
                (state_hbm, state),
                (body_hbm.at[0:CHUNK], body_op.at[0:CHUNK]),
                (flux_x_hbm, flux.at[0]),
                (flux_y_hbm, flux.at[1]),
                (viscosity_hbm, viscosity),
                (flux_z_hbm, flux.at[2]),
                (body_hbm.at[CHUNK:], body_op.at[CHUNK:]),
                (far_hbm, far_op),
                (edge_hbm, edge),
                (mortar_hbm, mortar_op),
            )
        )
    ]
    for load in loads:
        load.start()

    def remote(origin, target, k, row, column):
        return pltpu.make_async_remote_copy(
            src_ref=origin,
            dst_ref=target,
            send_sem=send_sem.at[k],
            recv_sem=recv_sem.at[k],
            device_id=(row, column),
            device_id_type=MESH,
        )

    from_left = inbox.at[0:MSG]
    from_right = inbox.at[MSG : 2 * MSG]
    from_before = inbox.at[2 * MSG : 3 * MSG]
    from_after = inbox.at[3 * MSG : 4 * MSG]
    go_right = remote(message.at[1], from_left, 0, me + 1, place)
    go_left = remote(message.at[0], from_right, 1, me - 1, place)
    go_after = remote(message.at[3], from_before, 2, me, after)
    go_before = remote(message.at[2], from_after, 3, me, before)
    tail = message.at[own, TAIL:]
    row_after = remote(tail, mortar_in.at[4 * MSG : 4 * MSG + HEAD], 4, me, after)
    row_before = remote(
        tail, mortar_in.at[4 * MSG + HEAD : 4 * MSG + 2 * HEAD], 5, me, before
    )

    pieces = []
    for k, (start, stop) in enumerate(((0, HEAD), (HEAD, MSG))):

        def box_at(part):
            return mortar_in.at[part * MSG + start : part * MSG + stop]

        pieces.append(
            (
                remote(message.at[own, start:stop], box_at(1), 6 + k, other_row, across),
                remote(box_at(1), box_at(2), 8 + k, me, after),
                remote(box_at(1), box_at(3), 10 + k, me, before),
            )
        )

    keep = pltpu.make_async_copy(message.at[own], mortar_in.at[0:MSG], local_sem.at[0])
    end_slot = pl.multiple_of(jnp.where(me == 0, 0, MSG), 8)
    close = pltpu.make_async_copy(message.at[4], inbox.at[pl.ds(end_slot, MSG)], local_sem.at[1])

    loads[0].wait()

    def pair(k):
        return pl.ds(pl.multiple_of(k * 2 * LANES, 2 * LANES), 2 * LANES)

    def one(v):
        return pl.ds(pl.multiple_of(v * LANES, LANES), LANES)

    pairs = (NV + 1) // 2

    def split_one(v, carry):
        whole = jnp.concatenate(
            [state[v], jnp.zeros((BODY_PAD - BODY, LANES), jnp.float32)], axis=0
        )
        put_box(box, one(v), whole)
        return carry

    lax.fori_loop(0, NV, split_one, 0)
    for load in loads[1:6]:
        load.wait()

    def find_speed(d, carry):
        largest = jnp.float32(0.0)
        for row in range(NV):
            entry = jnp.abs(flux[d, row, 0])
            for column in range(1, NV):
                entry = entry + jnp.abs(flux[d, row, column])
            largest = jnp.maximum(largest, entry)
        speed[d] = half_gain * largest
        return carry

    lax.fori_loop(0, 3, find_speed, 0)

    def make_message(origin, base, d, end, v, target, face):
        gain = jnp.where(end == 1, half_gain, -half_gain)
        at = pl.multiple_of(base, 8)
        lanes = one(v)
        mixed = speed[d] * origin[pl.ds(at, HEAD), lanes]
        for w in range(NV):
            mixed = mixed + (gain * flux[d, v, w]) * origin[pl.ds(at, HEAD), columns(w)]
        part = viscosity[v] * origin[pl.ds(pl.multiple_of(at + HEAD, 8), MSG), lanes]
        target[face, :HEAD, lanes] = part[:HEAD] + mixed
        target[face, HEAD:, lanes] = part[HEAD:]

    def send_face(face, carry):
        def make(v, carry):
            make_message(local, face * BLOCK, face // 2, lax.rem(face, 2), v, message, face)
            return carry

        lax.fori_loop(0, NV, make, 0)

        @pl.when(face == 1)
        def _():
            pl.semaphore_wait(barrier, jnp.where(is_mortar, 4, jnp.where(is_end, 3, 4)))

            @pl.when(is_mortar)
            def _():
                for send, _, _ in pieces:
                    send.start()
                row_after.start()
                row_before.start()
                keep.start()

            @pl.when(has_right)
            def _():
                go_right.start()

            @pl.when(has_left)
            def _():
                go_left.start()

        @pl.when(face == 3)
        def _():
            go_after.start()
            go_before.start()

        return carry

    def close_end():
        at = pl.multiple_of(jnp.where(me == 0, 0, BLOCK), 8)

        def close_one(v, carry):
            message[4, :HEAD, one(v)] = (half_gain * half_gain * viscosity[v]) * local[
                pl.ds(at, HEAD), one(v)
            ]
            message[4, HEAD:, one(v)] = jnp.zeros((MSG - HEAD, LANES), jnp.float32)
            return carry

        lax.fori_loop(0, NV, close_one, 0)
        close.start()

    def chunk_of(c, carry):
        rows = pl.ds(pl.multiple_of(c * CHUNK, 16), CHUNK)

        @pl.when(c == 1)
        def _():
            loads[6].wait()

        def local_pair(k, carry):
            lanes = pair(k)
            local[rows, lanes] = jnp.dot(
                body_op[rows, :], box[:, lanes], preferred_element_type=jnp.float32
            )
            return carry

        lax.fori_loop(0, pairs, local_pair, 0)

        @pl.when(c < 2)
        def _():
            lax.fori_loop(2 * c, 2 * c + 2, send_face, 0)

        @pl.when(jnp.logical_and(c == 1, is_end))
        def _():
            close_end()

        return carry

    lax.fori_loop(0, TABLE // CHUNK, chunk_of, 0)

    def make_inner(k, carry):
        end, v = k // NV, lax.rem(k, NV)
        make_message(local, Z_FACE + end * BLOCK, 2, end, v, z_message, end)
        return carry

    lax.fori_loop(0, 2 * NV, make_inner, 0)
    lane = lax.broadcasted_iota(jnp.int32, (MSG, LANES), 1)

    def fill_z(v, carry):
        lanes = one(v)
        closing = half_gain * half_gain * viscosity[v]
        blank = jnp.zeros((MSG - HEAD, LANES), jnp.float32)
        sides = []
        for end, (edge_lane, by) in enumerate(((0, 1), (LANES - 1, LANES - 1))):
            at = Z_FACE + end * BLOCK
            outside = jnp.concatenate([closing * local[at : at + HEAD, lanes], blank], axis=0)
            inside = pltpu.roll(z_message[1 - end, :, lanes], by, 1)
            sides.append(jnp.where(lane == edge_lane, outside, inside))
        put_box(far_box, lanes, jnp.concatenate(sides, axis=0))
        return carry

    loads[8].wait()
    rows_at_once = 24

    def mix_rows(k, carry):
        rows = pl.ds(pl.multiple_of(k * rows_at_once, 8), rows_at_once)
        weight = -speed[0] * edge[0, rows]
        for d in range(1, 3):
            weight = weight - speed[d] * edge[d, rows]

        def mix(v, carry):
            lanes = one(v)
            at = pl.ds(pl.multiple_of(OWN + 3 * BODY + k * rows_at_once, 8), rows_at_once)
            mixed = weight * state[v, rows] + viscosity[v] * local[at, lanes]
            for d in range(3):
                at = pl.ds(pl.multiple_of(OWN + d * BODY + k * rows_at_once, 8), rows_at_once)
                for w in range(NV):
                    mixed = mixed - flux[d, v, w] * local[at, columns(w)]
            total[rows, lanes] = mixed
            return carry

        return lax.fori_loop(0, NV, mix, carry)

    lax.fori_loop(0, BODY // rows_at_once, mix_rows, 0)

    loads[7].wait()
    loads[9].wait()

    def take_along():
        @pl.when(is_mortar)
        def _():
            for send, up, down in pieces:
                send.wait_recv()
                up.start()
                down.start()

        go_after.wait()
        go_before.wait()

    def take_axis():
        @pl.when(has_right)
        def _():
            go_right.wait_send()
            remote(message.at[0], from_right, 1, me + 1, place).wait_recv()

        @pl.when(has_left)
        def _():
            go_left.wait_send()
            remote(message.at[1], from_left, 0, me - 1, place).wait_recv()

        @pl.when(is_end)
        def _():
            close.wait()

        @pl.when(is_mortar)
        def _():
            for send, up, down in pieces:
                send.wait_send()
                up.wait()
                down.wait()
            row_after.wait()
            row_before.wait()
            keep.wait()
            straight_low = jnp.where(is_rotor, odd[0], 1 - odd[0])

            def fill_mortar(v, carry):
                put_box(mortar_box, one(v), mortar_in[:, one(v)])
                return carry

            lax.fori_loop(0, NV, fill_mortar, 0)

            def stand_pair(k, carry):
                lanes = pair(k)
                stand_in[:, lanes] = jnp.dot(
                    mortar_op[straight_low], mortar_box[:, lanes], preferred_element_type=jnp.float32
                )
                return carry

            lax.fori_loop(0, pairs, stand_pair, 0)
            slot_rows = pl.ds(pl.multiple_of(own * MSG, 8), MSG)
            for v in range(NV):
                inbox[slot_rows, columns(v)] = stand_in[:MSG, columns(v)]

    def add_far(stage, carry):
        d = 2 - stage

        @pl.when(stage == 0)
        def _():
            lax.fori_loop(0, NV, fill_z, 0)

        @pl.when(stage == 1)
        def _():
            take_along()

        @pl.when(stage == 2)
        def _():
            take_axis()

        @pl.when(stage > 0)
        def _():
            first_row = pl.multiple_of(d * 2 * MSG, 8)

            def fill(v, carry):
                put_box(far_box, one(v), inbox[pl.ds(first_row, 2 * MSG), one(v)])
                return carry

            lax.fori_loop(0, NV, fill, 0)

        def add(k, carry):
            lanes = pair(k)
            term = jnp.dot(far_op[d], far_box[:, lanes], preferred_element_type=jnp.float32)
            total[:, lanes] += term[:BODY]
            return carry

        return lax.fori_loop(0, pairs, add, carry)

    lax.fori_loop(0, 3, add_far, 0)
    store = pltpu.make_async_copy(total.at[:, 0:WIDE], residual_hbm, local_sem.at[2])
    store.start()
    store.wait()


def finish(state, register, residual, state_new, register_new):
    for v in range(NV):
        fresh = section_a * register[v] + residual[:, columns(v)]
        register_new[v] = fresh
        state_new[v] = state[v] + (section_b * step_size) * fresh


def on_device(counts, tables, state, register, flux_x, flux_y, flux_z, viscosity, mortar_partner):
    axial_count, sectors = counts
    body, far, mortar, edge = tables
    flat = state.reshape((NV, BODY, LANES))
    flat_register = register.reshape((NV, BODY, LANES))
    vmem = pl.BlockSpec(memory_space=pltpu.VMEM)
    hbm = pl.BlockSpec(memory_space=pltpu.HBM)
    smem = pl.BlockSpec(memory_space=pltpu.SMEM)
    limit = 48 * 1024 * 1024

    shift = lax.rem(mortar_partner[0, 0] - lax.axis_index("sector") + sectors, sectors)

    def run(which):
        return pl.pallas_call(
            functools.partial(exchange, which, counts),
            out_shape=jax.ShapeDtypeStruct((BODY, WIDE), jnp.float32),
            in_specs=[smem] + [hbm] * 9,
            out_specs=hbm,
            scratch_shapes=[
                pltpu.VMEM((NV, BODY, LANES), jnp.float32),
                pltpu.VMEM(body.shape, jnp.bfloat16),
                pltpu.VMEM(far.shape, jnp.bfloat16),
                pltpu.VMEM(mortar.shape, jnp.bfloat16),
                pltpu.VMEM(edge.shape, jnp.float32),
                pltpu.SMEM((3, NV, NV), jnp.float32),
                pltpu.SMEM((NV,), jnp.float32),
                pltpu.SMEM((3,), jnp.float32),
                pltpu.VMEM((5, MSG, WIDE), jnp.float32),
                pltpu.VMEM((3 * BODY_PAD, ROOM), jnp.bfloat16),
                pltpu.VMEM((4 * MSG, WIDE), jnp.float32),
                pltpu.VMEM((MORT_K, WIDE), jnp.float32),
                pltpu.VMEM((3 * MORT_K, ROOM), jnp.bfloat16),
                pltpu.VMEM((80, ROOM), jnp.float32),
                pltpu.VMEM((2, MSG, WIDE), jnp.float32),
                pltpu.VMEM((6 * MSG, ROOM), jnp.bfloat16),
                pltpu.VMEM((TABLE, ROOM), jnp.float32),
                pltpu.VMEM((BODY, ROOM), jnp.float32),
                pltpu.SemaphoreType.DMA((10,)),
                pltpu.SemaphoreType.DMA((3,)),
                pltpu.SemaphoreType.DMA((12,)),
                pltpu.SemaphoreType.DMA((12,)),
            ],
            compiler_params=pltpu.CompilerParams(
                collective_id=which, has_side_effects=True, vmem_limit_bytes=limit
            ),
            name=f"exchange_{which}",
        )

    residual = lax.switch(
        shift // 2,
        [run(which) for which in range(sectors // 2)],
        lax.rem(shift, 2).reshape((1,)),
        flat,
        body,
        far,
        mortar,
        edge,
        flux_x,
        flux_y,
        flux_z,
        viscosity,
    )

    whole = jax.ShapeDtypeStruct((NV, BODY, LANES), jnp.float32)
    state_new, register_new = pl.pallas_call(
        finish,
        out_shape=(whole, whole),
        in_specs=[vmem] * 3,
        out_specs=(vmem, vmem),
        name="finish",
    )(flat, flat_register, residual)
    return (state_new.reshape(state.shape), register_new.reshape(state.shape))


def solution(mesh):
    counts = (mesh.shape["axial"], mesh.shape["sector"])
    face, body, far, mortar = operators()
    edge = np.zeros((3, BODY, LANES), np.float32)
    ends = np.zeros(NN)
    ends[0] = ends[-1] = 1.0
    for d in range(3):
        edge[d] = np.diag(along(np.diag(ends), d))[:, None]
    tables = tuple(
        jnp.asarray(table)
        for table in (
            thirds(np.concatenate([face, body])),
            thirds(far),
            thirds(mortar),
            edge,
        )
    )
    spec = P(None, None, None, None, "axial", "sector", None)
    return jax.shard_map(
        functools.partial(on_device, counts, tables),
        mesh=mesh,
        in_specs=(spec, spec, P(), P(), P(), P(), P(None, "sector")),
        out_specs=(spec, spec),
        check_vma=False,
    )
```

```python
import functools

import jax
import jax.numpy as jnp
import numpy as np
from jax import lax
from jax.experimental import pallas as pl
from jax.experimental.pallas import tpu as pltpu
from jax.sharding import PartitionSpec as P

NODES = (
    -1.0,
    -0.7650553239294647,
    -0.2852315164806451,
    0.2852315164806451,
    0.7650553239294647,
    1.0,
)
WEIGHTS = (
    1.0 / 15.0,
    0.378474956297847,
    0.5548583770354863,
    0.5548583770354863,
    0.378474956297847,
    1.0 / 15.0,
)
half_gain = 7.5
step_size = 0.01
section_a = -0.4178904745
section_b = 1.5306374668
MESH = pl.DeviceIdType.MESH

NV = 5
NN = 6
FACE = NN * NN
BODY = NN * FACE
BODY_PAD = 224
LANES = 128
WIDE = NV * LANES
ROOM = WIDE + LANES
MSG = 2 * FACE
HEAD = 40
BLOCK = HEAD + MSG
TAIL = 32
MORT_K = 368
Z_FACE = 4 * BLOCK
OWN = 6 * BLOCK
TABLE = OWN + 4 * BODY
CHUNK = 256


def basis_tables():
    points = np.array(NODES)
    weights = np.array(WEIGHTS)
    count = points.shape[0]
    barycentric = np.array(
        [
            1.0
            / np.prod([points[first] - points[other] for other in range(count) if other != first])
            for first in range(count)
        ]
    )
    derivative = np.zeros((count, count))
    for target in range(count):
        for source in range(count):
            if source != target:
                derivative[target, source] = (
                    barycentric[source] / barycentric[target] / (points[target] - points[source])
                )
        derivative[target, target] = -np.sum(derivative[target])

    def lagrange(places):
        result = np.ones((count, count))
        for column in range(count):
            for other in range(count):
                if other != column:
                    result[:, column] *= (places - points[other]) / (points[column] - points[other])
        return result

    lower_map = lagrange((points - 1.0) / 2.0)
    upper_map = lagrange((points + 1.0) / 2.0)
    back_lower = 0.5 * lower_map.T * weights[None, :] / weights[:, None]
    back_upper = 0.5 * upper_map.T * weights[None, :] / weights[:, None]
    return derivative, lower_map, upper_map, back_lower, back_upper


def along(matrix, dimension):
    parts = [np.eye(NN)] * 3
    parts[dimension] = matrix
    return np.kron(np.kron(parts[0], parts[1]), parts[2])


def operators():
    derivative, lower_map, upper_map, back_lower, back_upper = basis_tables()
    eye = np.eye(NN)
    first, last = eye[:1], eye[-1:]

    body = np.zeros((4 * BODY, BODY_PAD))
    second = np.zeros((BODY, BODY))
    for d in range(3):
        own = derivative + half_gain * (first.T @ first - last.T @ last)
        twice = derivative @ own + half_gain * (
            first.T @ derivative[:1] - last.T @ derivative[-1:]
        )
        body[d * BODY : (d + 1) * BODY, :BODY] = along(own, d)
        second += along(twice, d)
    body[3 * BODY :, :BODY] = second

    face = np.zeros((6 * BLOCK, BODY_PAD))
    far = np.zeros((3, BODY_PAD, 2 * MSG))
    for d in range(3):
        for end in range(2):
            row = first if end == 0 else last
            slope = derivative[:1] if end == 0 else derivative[-1:]
            sign = 1.0 if end == 0 else -1.0
            at = (2 * d + end) * BLOCK
            trace = along(row, d)
            face[at : at + FACE, :BODY] = trace
            face[at + HEAD : at + HEAD + FACE, :BODY] = sign * half_gain * along(slope, d)
            face[at + HEAD + FACE : at + BLOCK, :BODY] = half_gain * trace
            to = end * MSG
            column = derivative[:, :1] if end == 0 else derivative[:, -1:]
            far[d, :BODY, to : to + FACE] = trace.T
            far[d, :BODY, to + FACE : to + MSG] = -sign * along(column, d)

    low = back_lower @ upper_map
    high = back_upper @ lower_map
    same = back_lower @ lower_map + back_upper @ upper_map
    less = same - 2.0 * eye

    def on_face(matrix):
        return np.kron(matrix, eye)

    mortar = np.zeros((2, 80, MORT_K))
    b, c = slice(0, FACE), slice(FACE, MSG)
    skip = FACE - TAIL
    for straight_low in range(2):

        def put(rows, at, matrix):
            mortar[straight_low, rows, at : at + FACE] = on_face(matrix)

        low_at, high_at = (MSG, 3 * MSG) if straight_low else (2 * MSG, MSG)
        put(b, 0, eye - same)
        put(b, FACE, half_gain * (less @ less - low @ high - high @ low))
        put(c, FACE, same - eye)
        for matrix, at in ((low, low_at), (high, high_at)):
            put(b, at, matrix)
            put(b, at + FACE, half_gain * (less @ matrix - matrix @ less))
            put(c, at + FACE, matrix)
        put(b, 4 * MSG + skip, -half_gain * (low @ low))
        put(b, 4 * MSG + HEAD + skip, -half_gain * (high @ high))
    return face, body, far, mortar


def thirds(matrix):
    high = np.asarray(matrix, np.float32).astype(jnp.bfloat16)
    low = (matrix - high.astype(np.float64)).astype(np.float32).astype(jnp.bfloat16)
    return np.concatenate([high, high, low], axis=-1)


def put_box(box, lanes, value):
    rows = value.shape[0]
    high = value.astype(jnp.bfloat16)
    box[0:rows, lanes] = high
    box[rows : 2 * rows, lanes] = (value - high.astype(jnp.float32)).astype(jnp.bfloat16)
    box[2 * rows : 3 * rows, lanes] = high


def place_of(counts):
    axial_count = counts[0]
    half = axial_count // 2
    me = lax.axis_index("axial")
    is_rotor = me == half - 1
    is_mortar = jnp.logical_or(me == half - 1, me == half)
    has_left = jnp.logical_and(me != 0, me != half)
    has_right = jnp.logical_and(me != axial_count - 1, me != half - 1)
    return me, is_rotor, is_mortar, has_left, has_right


def columns(v):
    return slice(v * LANES, (v + 1) * LANES)


def exchange(
    shift,
    counts,
    odd,
    state_hbm,
    body_hbm,
    far_hbm,
    mortar_hbm,
    edge_hbm,
    flux_x_hbm,
    flux_y_hbm,
    flux_z_hbm,
    viscosity_hbm,
    residual_hbm,
    state,
    body_op,
    far_op,
    mortar_op,
    edge,
    flux,
    viscosity,
    speed,
    message,
    box,
    inbox,
    mortar_in,
    mortar_box,
    stand_in,
    z_message,
    far_box,
    local,
    total,
    load_sem,
    local_sem,
    send_sem,
    recv_sem,
):
    axial_count, sectors = counts
    half = axial_count // 2
    me, is_rotor, is_mortar, has_left, has_right = place_of(counts)
    is_end = jnp.logical_or(me == 0, me == axial_count - 1)
    place = lax.axis_index("sector")
    after = lax.rem(place + 1, sectors)
    before = lax.rem(place + sectors - 1, sectors)
    turn = 2 * shift + 1
    across = lax.rem(
        place + jnp.where(is_rotor, turn % sectors, (sectors - turn) % sectors), sectors
    )
    other_row = jnp.where(is_rotor, half, half - 1)
    own = jnp.where(is_rotor, 1, 0)

    barrier = pltpu.get_barrier_semaphore()

    def greet(row, column):
        pl.semaphore_signal(barrier, inc=1, device_id=(row, column), device_id_type=MESH)

    @pl.when(is_mortar)
    def _():
        greet(other_row, across)

    greet(me, after)
    greet(me, before)

    @pl.when(has_left)
    def _():
        greet(me - 1, place)

    @pl.when(has_right)
    def _():
        greet(me + 1, place)

    loads = [
        pltpu.make_async_copy(origin, target, load_sem.at[k])
        for k, (origin, target) in enumerate(
            (
                (state_hbm, state),
                (body_hbm.at[0:CHUNK], body_op.at[0:CHUNK]),
                (flux_x_hbm, flux.at[0]),
                (flux_y_hbm, flux.at[1]),
                (viscosity_hbm, viscosity),
                (flux_z_hbm, flux.at[2]),
                (body_hbm.at[CHUNK:], body_op.at[CHUNK:]),
                (far_hbm, far_op),
                (edge_hbm, edge),
                (mortar_hbm, mortar_op),
            )
        )
    ]
    for load in loads:
        load.start()

    def remote(origin, target, k, row, column):
        return pltpu.make_async_remote_copy(
            src_ref=origin,
            dst_ref=target,
            send_sem=send_sem.at[k],
            recv_sem=recv_sem.at[k],
            device_id=(row, column),
            device_id_type=MESH,
        )

    from_left = inbox.at[0:MSG]
    from_right = inbox.at[MSG : 2 * MSG]
    from_before = inbox.at[2 * MSG : 3 * MSG]
    from_after = inbox.at[3 * MSG : 4 * MSG]
    go_right = remote(message.at[1], from_left, 0, me + 1, place)
    go_left = remote(message.at[0], from_right, 1, me - 1, place)
    go_after = remote(message.at[3], from_before, 2, me, after)
    go_before = remote(message.at[2], from_after, 3, me, before)
    tail = message.at[own, TAIL:]
    row_after = remote(tail, mortar_in.at[4 * MSG : 4 * MSG + HEAD], 4, me, after)
    row_before = remote(
        tail, mortar_in.at[4 * MSG + HEAD : 4 * MSG + 2 * HEAD], 5, me, before
    )

    pieces = []
    for k, (start, stop) in enumerate(((0, HEAD), (HEAD, MSG))):

        def box_at(part):
            return mortar_in.at[part * MSG + start : part * MSG + stop]

        pieces.append(
            (
                remote(message.at[own, start:stop], box_at(1), 6 + k, other_row, across),
                remote(box_at(1), box_at(2), 8 + k, me, after),
                remote(box_at(1), box_at(3), 10 + k, me, before),
            )
        )

    keep = pltpu.make_async_copy(message.at[own], mortar_in.at[0:MSG], local_sem.at[0])
    end_slot = pl.multiple_of(jnp.where(me == 0, 0, MSG), 8)
    close = pltpu.make_async_copy(message.at[4], inbox.at[pl.ds(end_slot, MSG)], local_sem.at[1])

    loads[0].wait()

    def pair(k):
        return pl.ds(pl.multiple_of(k * 2 * LANES, 2 * LANES), 2 * LANES)

    def one(v):
        return pl.ds(pl.multiple_of(v * LANES, LANES), LANES)

    pairs = (NV + 1) // 2

    def split_one(v, carry):
        whole = jnp.concatenate(
            [state[v], jnp.zeros((BODY_PAD - BODY, LANES), jnp.float32)], axis=0
        )
        put_box(box, one(v), whole)
        return carry

    lax.fori_loop(0, NV, split_one, 0)
    for load in loads[1:6]:
        load.wait()

    def find_speed(d, carry):
        largest = jnp.float32(0.0)
        for row in range(NV):
            entry = jnp.abs(flux[d, row, 0])
            for column in range(1, NV):
                entry = entry + jnp.abs(flux[d, row, column])
            largest = jnp.maximum(largest, entry)
        speed[d] = half_gain * largest
        return carry

    lax.fori_loop(0, 3, find_speed, 0)

    def make_message(origin, base, d, end, v, target, face):
        gain = jnp.where(end == 1, half_gain, -half_gain)
        at = pl.multiple_of(base, 8)
        lanes = one(v)
        mixed = speed[d] * origin[pl.ds(at, HEAD), lanes]
        for w in range(NV):
            mixed = mixed + (gain * flux[d, v, w]) * origin[pl.ds(at, HEAD), columns(w)]
        part = viscosity[v] * origin[pl.ds(pl.multiple_of(at + HEAD, 8), MSG), lanes]
        target[face, :HEAD, lanes] = part[:HEAD] + mixed
        target[face, HEAD:, lanes] = part[HEAD:]

    def send_face(face, carry):
        def make(v, carry):
            make_message(local, face * BLOCK, face // 2, lax.rem(face, 2), v, message, face)
            return carry

        lax.fori_loop(0, NV, make, 0)

        @pl.when(face == 1)
        def _():
            pl.semaphore_wait(barrier, jnp.where(is_mortar, 4, jnp.where(is_end, 3, 4)))

            @pl.when(is_mortar)
            def _():
                for send, _, _ in pieces:
                    send.start()
                row_after.start()
                row_before.start()
                keep.start()

            @pl.when(has_right)
            def _():
                go_right.start()

            @pl.when(has_left)
            def _():
                go_left.start()

        @pl.when(face == 3)
        def _():
            go_after.start()
            go_before.start()

        return carry

    def close_end():
        at = pl.multiple_of(jnp.where(me == 0, 0, BLOCK), 8)

        def close_one(v, carry):
            message[4, :HEAD, one(v)] = (half_gain * half_gain * viscosity[v]) * local[
                pl.ds(at, HEAD), one(v)
            ]
            message[4, HEAD:, one(v)] = jnp.zeros((MSG - HEAD, LANES), jnp.float32)
            return carry

        lax.fori_loop(0, NV, close_one, 0)
        close.start()

    def chunk_of(c, carry):
        rows = pl.ds(pl.multiple_of(c * CHUNK, 16), CHUNK)

        @pl.when(c == 1)
        def _():
            loads[6].wait()

        local[rows, 0:WIDE] = jnp.dot(
            body_op[rows, :], box[:, 0:WIDE], preferred_element_type=jnp.float32
        )

        @pl.when(c < 2)
        def _():
            lax.fori_loop(2 * c, 2 * c + 2, send_face, 0)

        @pl.when(jnp.logical_and(c == 1, is_end))
        def _():
            close_end()

        return carry

    lax.fori_loop(0, TABLE // CHUNK, chunk_of, 0)

    def make_inner(k, carry):
        end, v = k // NV, lax.rem(k, NV)
        make_message(local, Z_FACE + end * BLOCK, 2, end, v, z_message, end)
        return carry

    lax.fori_loop(0, 2 * NV, make_inner, 0)
    lane = lax.broadcasted_iota(jnp.int32, (MSG, LANES), 1)

    def fill_z(v, carry):
        lanes = one(v)
        closing = half_gain * half_gain * viscosity[v]
        blank = jnp.zeros((MSG - HEAD, LANES), jnp.float32)
        sides = []
        for end, (edge_lane, by) in enumerate(((0, 1), (LANES - 1, LANES - 1))):
            at = Z_FACE + end * BLOCK
            outside = jnp.concatenate([closing * local[at : at + HEAD, lanes], blank], axis=0)
            inside = pltpu.roll(z_message[1 - end, :, lanes], by, 1)
            sides.append(jnp.where(lane == edge_lane, outside, inside))
        put_box(far_box, lanes, jnp.concatenate(sides, axis=0))
        return carry

    loads[8].wait()
    rows_at_once = 24

    def mix_rows(k, carry):
        rows = pl.ds(pl.multiple_of(k * rows_at_once, 8), rows_at_once)
        weight = -speed[0] * edge[0, rows]
        for d in range(1, 3):
            weight = weight - speed[d] * edge[d, rows]

        def mix(v, carry):
            lanes = one(v)
            at = pl.ds(pl.multiple_of(OWN + 3 * BODY + k * rows_at_once, 8), rows_at_once)
            mixed = weight * state[v, rows] + viscosity[v] * local[at, lanes]
            for d in range(3):
                at = pl.ds(pl.multiple_of(OWN + d * BODY + k * rows_at_once, 8), rows_at_once)
                for w in range(NV):
                    mixed = mixed - flux[d, v, w] * local[at, columns(w)]
            total[rows, lanes] = mixed
            return carry

        return lax.fori_loop(0, NV, mix, carry)

    lax.fori_loop(0, BODY // rows_at_once, mix_rows, 0)

    loads[7].wait()
    loads[9].wait()

    def take_along():
        @pl.when(is_mortar)
        def _():
            for send, up, down in pieces:
                send.wait_recv()
                up.start()
                down.start()

        go_after.wait()
        go_before.wait()

    def take_axis():
        @pl.when(has_right)
        def _():
            go_right.wait_send()
            remote(message.at[0], from_right, 1, me + 1, place).wait_recv()

        @pl.when(has_left)
        def _():
            go_left.wait_send()
            remote(message.at[1], from_left, 0, me - 1, place).wait_recv()

        @pl.when(is_end)
        def _():
            close.wait()

        @pl.when(is_mortar)
        def _():
            for send, up, down in pieces:
                send.wait_send()
                up.wait()
                down.wait()
            row_after.wait()
            row_before.wait()
            keep.wait()
            straight_low = jnp.where(is_rotor, odd[0], 1 - odd[0])

            def fill_mortar(v, carry):
                put_box(mortar_box, one(v), mortar_in[:, one(v)])
                return carry

            lax.fori_loop(0, NV, fill_mortar, 0)

            def stand_pair(k, carry):
                lanes = pair(k)
                stand_in[:, lanes] = jnp.dot(
                    mortar_op[straight_low], mortar_box[:, lanes], preferred_element_type=jnp.float32
                )
                return carry

            lax.fori_loop(0, pairs, stand_pair, 0)
            slot_rows = pl.ds(pl.multiple_of(own * MSG, 8), MSG)
            for v in range(NV):
                inbox[slot_rows, columns(v)] = stand_in[:MSG, columns(v)]

    def add_far(stage, carry):
        d = 2 - stage

        @pl.when(stage == 0)
        def _():
            lax.fori_loop(0, NV, fill_z, 0)

        @pl.when(stage == 1)
        def _():
            take_along()

        @pl.when(stage == 2)
        def _():
            take_axis()

        @pl.when(stage > 0)
        def _():
            first_row = pl.multiple_of(d * 2 * MSG, 8)

            def fill(v, carry):
                put_box(far_box, one(v), inbox[pl.ds(first_row, 2 * MSG), one(v)])
                return carry

            lax.fori_loop(0, NV, fill, 0)

        term = jnp.dot(far_op[d], far_box[:, 0:WIDE], preferred_element_type=jnp.float32)
        total[:, 0:WIDE] += term[:BODY]
        return carry

    lax.fori_loop(0, 3, add_far, 0)
    store = pltpu.make_async_copy(total.at[:, 0:WIDE], residual_hbm, local_sem.at[2])
    store.start()
    store.wait()


def finish(state, register, residual, state_new, register_new):
    for v in range(NV):
        fresh = section_a * register[v] + residual[:, columns(v)]
        register_new[v] = fresh
        state_new[v] = state[v] + (section_b * step_size) * fresh


def on_device(counts, tables, state, register, flux_x, flux_y, flux_z, viscosity, mortar_partner):
    axial_count, sectors = counts
    body, far, mortar, edge = tables
    flat = state.reshape((NV, BODY, LANES))
    flat_register = register.reshape((NV, BODY, LANES))
    vmem = pl.BlockSpec(memory_space=pltpu.VMEM)
    hbm = pl.BlockSpec(memory_space=pltpu.HBM)
    smem = pl.BlockSpec(memory_space=pltpu.SMEM)
    limit = 48 * 1024 * 1024

    shift = lax.rem(mortar_partner[0, 0] - lax.axis_index("sector") + sectors, sectors)

    def run(which):
        return pl.pallas_call(
            functools.partial(exchange, which, counts),
            out_shape=jax.ShapeDtypeStruct((BODY, WIDE), jnp.float32),
            in_specs=[smem] + [hbm] * 9,
            out_specs=hbm,
            scratch_shapes=[
                pltpu.VMEM((NV, BODY, LANES), jnp.float32),
                pltpu.VMEM(body.shape, jnp.bfloat16),
                pltpu.VMEM(far.shape, jnp.bfloat16),
                pltpu.VMEM(mortar.shape, jnp.bfloat16),
                pltpu.VMEM(edge.shape, jnp.float32),
                pltpu.SMEM((3, NV, NV), jnp.float32),
                pltpu.SMEM((NV,), jnp.float32),
                pltpu.SMEM((3,), jnp.float32),
                pltpu.VMEM((5, MSG, WIDE), jnp.float32),
                pltpu.VMEM((3 * BODY_PAD, ROOM), jnp.bfloat16),
                pltpu.VMEM((4 * MSG, WIDE), jnp.float32),
                pltpu.VMEM((MORT_K, WIDE), jnp.float32),
                pltpu.VMEM((3 * MORT_K, ROOM), jnp.bfloat16),
                pltpu.VMEM((80, ROOM), jnp.float32),
                pltpu.VMEM((2, MSG, WIDE), jnp.float32),
                pltpu.VMEM((6 * MSG, ROOM), jnp.bfloat16),
                pltpu.VMEM((TABLE, ROOM), jnp.float32),
                pltpu.VMEM((BODY, ROOM), jnp.float32),
                pltpu.SemaphoreType.DMA((10,)),
                pltpu.SemaphoreType.DMA((3,)),
                pltpu.SemaphoreType.DMA((12,)),
                pltpu.SemaphoreType.DMA((12,)),
            ],
            compiler_params=pltpu.CompilerParams(
                collective_id=which, has_side_effects=True, vmem_limit_bytes=limit
            ),
            name=f"exchange_{which}",
        )

    residual = lax.switch(
        shift // 2,
        [run(which) for which in range(sectors // 2)],
        lax.rem(shift, 2).reshape((1,)),
        flat,
        body,
        far,
        mortar,
        edge,
        flux_x,
        flux_y,
        flux_z,
        viscosity,
    )

    whole = jax.ShapeDtypeStruct((NV, BODY, LANES), jnp.float32)
    state_new, register_new = pl.pallas_call(
        finish,
        out_shape=(whole, whole),
        in_specs=[vmem] * 3,
        out_specs=(vmem, vmem),
        name="finish",
    )(flat, flat_register, residual)
    return (state_new.reshape(state.shape), register_new.reshape(state.shape))


def solution(mesh):
    counts = (mesh.shape["axial"], mesh.shape["sector"])
    face, body, far, mortar = operators()
    edge = np.zeros((3, BODY, LANES), np.float32)
    ends = np.zeros(NN)
    ends[0] = ends[-1] = 1.0
    for d in range(3):
        edge[d] = np.diag(along(np.diag(ends), d))[:, None]
    tables = tuple(
        jnp.asarray(table)
        for table in (
            thirds(np.concatenate([face, body])),
            thirds(far),
            thirds(mortar),
            edge,
        )
    )
    spec = P(None, None, None, None, "axial", "sector", None)
    return jax.shard_map(
        functools.partial(on_device, counts, tables),
        mesh=mesh,
        in_specs=(spec, spec, P(), P(), P(), P(), P(None, "sector")),
        out_specs=(spec, spec),
        check_vma=False,
    )
```
